256 devices in a mesh: gx: 8 (over z_hi, x), gy: 32 (over z_lo, y, core).
Axes of the slice: x: 4, y: 4, z: 8 (z_hi: 2, z_lo: 4; z = z_hi * 4 + z_lo), core: 2. Of those that a mesh axis runs over, the one named last changes fastest.
Arguments:
- features: bfloat16 [100352, 512], P(('gx', 'gy')), may hold values from -24 to 24
- weight: bfloat16 [512, 2048], replicated, may hold values from -0.25 to 0.25
- cotangent: bfloat16 [100352, 2048], P(('gx', 'gy')), may hold values from -6 to 6
- pre_act: bfloat16 [100352, 2048], P(('gx', 'gy')), may hold values from -6 to 6
- bn_params: float32 [2, 2048], replicated, may hold values from 0.45 to 1.55
- master_weight: float32 [512, 2048], P(('gx', 'gy')), may hold values from -0.19 to 0.19
- weight_momentum: float32 [512, 2048], P(('gx', 'gy')), may hold values from -0.2 to 0.2
- bn_momentum: float32 [2, 2048], P(None, ('gx', 'gy')), may hold values from 0.6 to 1.6
Outputs:
- grad_input: bfloat16 [100352, 512], P(('gx', 'gy'))
- grad_skip: bfloat16 [100352, 2048], P(('gx', 'gy'))
- new_master: float32 [512, 2048], P(('gx', 'gy'))
- new_momentum: float32 [512, 2048], P(('gx', 'gy'))
- new_weight: bfloat16 [512, 2048], replicated
- new_bn_master: float32 [2, 2048], P(None, ('gx', 'gy'))
- new_bn_momentum: float32 [2, 2048], P(None, ('gx', 'gy'))
- new_bn: bfloat16 [2, 2048], replicated
The draws below stay inside these ranges and needn't reach their ends.
All inputs are finite; a program needn't handle non-finite values.
Results may differ from the reference program's by a relative error of at most 0.011.
Values may be sent and summed in bfloat16 or wider, within the bound.
No kernel may reach another device: no remote copies, remote signals or barrier semaphores. Data moves between devices by JAX's collectives and lax.ppermute only.
A program may use at most 64 MiB of HBM per device.

```python
import jax
import jax.numpy as jnp
from jax import lax

C = 2048
CB = 512
ROWS_DEV = 392
ROWS = 100352
N_GX = 8
N_GY = 32


def common_momentum(key):
    key = jax.random.fold_in(key, 71)
    return 0.05 * jnp.clip(jax.random.normal(key, (CB, C), jnp.float32), -4.0, 4.0)


def common_bn_momentum(key):
    key = jax.random.fold_in(key, 72)
    return jax.random.uniform(key, (2, C), jnp.float32, 0.6, 1.6)


def draw_weight_momentum(key, part):
    return common_momentum(key)


def draw_master_weight(key, part):
    shared = common_momentum(key)
    key = jax.random.fold_in(key, 3)
    noise_part = jnp.clip(jax.random.normal(key, (CB, C), jnp.float32), -4.0, 4.0)
    return 0.9 * shared + 0.0015 * noise_part


def draw_bn_momentum(key, part):
    return common_bn_momentum(key)


def draw_bn_params(key, part):
    shared = common_bn_momentum(key)
    key = jax.random.fold_in(key, 5)
    noise_part = jnp.clip(jax.random.normal(key, (2, C), jnp.float32), -4.0, 4.0)
    return 0.9 * shared + 0.02 * noise_part


def spiked(result, key, source, target, parts, factor):
    def block_of(axis_at):
        return (jnp.arange(result.shape[axis_at]) // (result.shape[axis_at] // parts)).reshape((-1,) + (1,) * (result.ndim - 1 - axis_at))

    one_side = jax.random.permutation(key, parts)[block_of(target)]
    second = (block_of(target) + parts // 2) % parts
    return jnp.where((block_of(source) == one_side) | (block_of(source) == second), factor * result, result)


def levels(stream_key, extent, cuts, low, high):
    factor_of, own = 1.0, jax.random.fold_in(stream_key, 6)
    for position, blocks in cuts:
        draws = jnp.exp(jax.random.uniform(jax.random.fold_in(own, position), (blocks,), jnp.float32, low / len(cuts), high / len(cuts)))
        factor_of = factor_of * jnp.repeat(draws, extent[position] // blocks).reshape([-1 if axis == position else 1 for axis in range(len(extent))])
    return factor_of


def bell_draw(own_key, extent, spread, reach, cuts=(), held_as=jnp.bfloat16):
    values = spread * jax.random.normal(own_key, extent, jnp.float32)
    if cuts:
        values = values * levels(own_key, extent, cuts, -0.22, 0.18)
    return jnp.clip(values, -reach, reach).astype(held_as)


def gaussian_with(rng, dims, spread, reach, shards, heavy, kind=jnp.bfloat16):
    entries = spread * jax.random.normal(rng, dims, jnp.float32)
    if shards:
        entries = entries * levels(rng, dims, shards, -0.22, 0.18)
    return jnp.clip(spiked(entries, jax.random.fold_in(rng, 3), *heavy), -reach, reach).astype(kind)


def setup_inputs(seed: int = 0) -> dict:
    streams_of = jax.random.split(jax.random.key(seed), 9)
    return {
        "features": gaussian_with(streams_of[0], (ROWS, CB), 1.0, 24.0, ((0, 256),), (0, 1, 256, 6.0)),
        "weight": bell_draw(streams_of[1], (CB, C), CB ** -0.5, 0.25),
        "cotangent": bell_draw(streams_of[2], (ROWS, C), 1.0, 6.0, ((0, 256),)),
        "pre_act": bell_draw(streams_of[3], (ROWS, C), 1.0, 6.0, ((0, 256),)),
        "bn_params": draw_bn_params(jax.random.fold_in(streams_of[8], 71), 0),
        "master_weight": draw_master_weight(jax.random.fold_in(streams_of[8], 71), 0),
        "weight_momentum": draw_weight_momentum(jax.random.fold_in(streams_of[8], 71), 0),
        "bn_momentum": draw_bn_momentum(jax.random.fold_in(streams_of[8], 71), 0),
    }


eps_norm = 1e-05
momentum_rate = 0.9
learn_rate = 4.0
trust_coef = 0.001
decay_rate = 5e-05

def regroup(array):
    width = array.shape[1]
    return array.reshape(N_GX, N_GY, ROWS_DEV, width).transpose(1, 0, 2, 3).reshape(N_GY, N_GX * ROWS_DEV, width)

def ungroup(array):
    width = array.shape[2]
    return array.reshape(N_GY, N_GX, ROWS_DEV, width).transpose(1, 0, 2, 3).reshape(N_GX * N_GY * ROWS_DEV, width)

def reference(features, weight, cotangent, pre_act, bn_params, master_weight, weight_momentum, bn_momentum):
    scale = bn_params[0]

    def group(carry, pieces):
        feat, cot, pre = pieces
        conv = jnp.dot(feat, weight, preferred_element_type=jnp.float32)
        mean = lax.optimization_barrier(jnp.mean(conv, axis=0))
        inv_std = lax.rsqrt(lax.optimization_barrier(jnp.mean(conv * conv, axis=0)) - mean * mean + eps_norm)
        normed = (conv - mean) * inv_std
        upstream = jnp.where(pre > 0, cot.astype(jnp.float32), jnp.float32(0.0))
        sum_b = lax.optimization_barrier(jnp.sum(upstream, axis=0))
        sum_g = lax.optimization_barrier(jnp.sum(upstream * normed, axis=0))
        count = jnp.float32(N_GX * ROWS_DEV)
        grad_conv = (scale * inv_std * (upstream - sum_b / count - normed * sum_g / count)).astype(jnp.bfloat16)
        grad_in = lax.dot_general(grad_conv, weight, (((1,), (1,)), ((), ())), preferred_element_type=jnp.float32)
        wgrad = carry[0] + lax.dot_general(feat, grad_conv, (((0,), (0,)), ((), ())), preferred_element_type=jnp.float32)
        bgrad = carry[1] + jnp.stack([sum_g, sum_b])
        return ((wgrad, bgrad), (grad_in.astype(jnp.bfloat16), upstream.astype(jnp.bfloat16)))
    start = (jnp.zeros((CB, C), jnp.float32), jnp.zeros((2, C), jnp.float32))
    (weight_grad, bn_grad), (grad_in, grad_skip) = lax.scan(group, start, (regroup(features), regroup(cotangent), regroup(pre_act)))
    w_sq = jnp.stack([jnp.sum(master_weight * master_weight), jnp.sum(bn_params[0] * bn_params[0]), jnp.sum(bn_params[1] * bn_params[1])])
    g_sq = jnp.stack([jnp.sum(weight_grad * weight_grad), jnp.sum(bn_grad[0] * bn_grad[0]), jnp.sum(bn_grad[1] * bn_grad[1])])
    w_norm = jnp.sqrt(w_sq)
    trust = trust_coef * w_norm / (jnp.sqrt(g_sq) + decay_rate * w_norm)
    new_momentum = momentum_rate * weight_momentum + learn_rate * trust[0] * (weight_grad + decay_rate * master_weight)
    new_master = master_weight - new_momentum
    new_bn_momentum = momentum_rate * bn_momentum + learn_rate * trust[1:3][:, None] * (bn_grad + decay_rate * bn_params)
    new_bn_master = bn_params - new_bn_momentum
    return (ungroup(grad_in), ungroup(grad_skip), new_master, new_momentum, new_master.astype(jnp.bfloat16), new_bn_master, new_bn_momentum, new_bn_master.astype(jnp.bfloat16))
```

```python
import jax
import jax.numpy as jnp
from jax import lax
from jax.sharding import Mesh, PartitionSpec as P

eps_norm = 1e-05
momentum_rate = 0.9
learn_rate = 4.0
trust_coef = 0.001
decay_rate = 5e-05

AXES = ("zh", "x", "zl", "y", "c")
SIZES = (2, 4, 4, 4, 2)
GX = ("zh", "x")
YZ = ("zh", "zl", "y")
BF = jnp.bfloat16
F32 = jnp.float32


def index_of(zh, x, zl, y, c):
    return (((zh * 4 + x) * 4 + zl) * 4 + y) * 2 + c


def pairs(move):
    out = []
    for zh in range(2):
        for x in range(4):
            for zl in range(4):
                for y in range(4):
                    for c in range(2):
                        out.append((index_of(zh, x, zl, y, c), index_of(*move(zh, x, zl, y, c))))
    return out


SIBLING = pairs(lambda zh, x, zl, y, c: (zh, x, zl, y, 1 - c))


def to_x(k):
    return pairs(lambda zh, x, zl, y, c: (zh, (x + k) % 4, zl, y, c))


def select(rows, x, c):
    t = lax.broadcasted_iota(jnp.int32, (rows, 512), 1)
    r = lax.broadcasted_iota(jnp.int32, (rows, 512), 0)
    cc = c ^ (t >> 8)
    xx = (x + (t >> 6)) & 3
    want = ((t >> 5) & 1) * 256 + xx * 64 + ((t >> 3) & 3) * 16 + ((t >> 1) & 3) * 4 + cc * 2 + (t & 1)
    return (r == want).astype(BF)


def hi_lo(v):
    hi = v.astype(BF)
    lo = (v - hi.astype(F32)).astype(BF)
    return hi, lo


def shards(features, weight, cotangent, pre_act, bn_params, master, momentum, bn_momentum):
    x = lax.axis_index("x")
    c = lax.axis_index("c")
    mine = lax.axis_index(AXES)
    rows = features.shape[0]
    count = jnp.float32(rows * 8)
    sel = select(512, x, c)
    own_bn = lax.dynamic_slice_in_dim(bn_params, mine * 8, 8, 1)

    conv = jnp.dot(features, weight, preferred_element_type=F32)
    up = jnp.where(pre_act > 0, cotangent, jnp.zeros_like(cotangent))
    upf = up.astype(F32)
    local = jnp.stack([jnp.sum(conv, 0), jnp.sum(conv * conv, 0), jnp.sum(upf, 0), jnp.sum(upf * conv, 0)])
    sent = jnp.broadcast_to(local.reshape(1, 8, 1024), (8, 8, 1024))
    got = lax.all_to_all(sent, GX, 0, 0, tiled=True)
    sums = jnp.sum(got, axis=0).reshape(4, 2048)
    mean = sums[0] / count
    inv_std = lax.rsqrt(sums[1] / count - mean * mean + eps_norm)
    sum_b = sums[2]
    sum_g = inv_std * (sums[3] - mean * sums[2])
    local_b = local[2]
    local_g = inv_std * (local[3] - mean * local[2])
    normed = (conv - mean) * inv_std
    grad_conv = (bn_params[0] * inv_std * (upf - sum_b / count - normed * sum_g / count)).astype(BF)
    grad_input = lax.dot_general(
        grad_conv, weight, (((1,), (1,)), ((), ())), preferred_element_type=F32
    ).astype(BF)

    feat = jnp.dot(features, sel, preferred_element_type=F32).astype(BF)
    g = lax.dot_general(feat, grad_conv, (((0,), (0,)), ((), ())), preferred_element_type=F32)
    bn_rows = jnp.stack([local_g, local_b]).reshape(2, 256, 8).transpose(1, 0, 2).reshape(512, 8).astype(BF)
    extra = lax.dot_general(sel, bn_rows, (((0,), (0,)), ((), ())), preferred_element_type=F32)
    g = jnp.concatenate([g, jnp.pad(extra, ((0, 0), (0, 120)))], axis=1)
    half = g[:256] + lax.ppermute(g[256:].astype(BF), AXES, SIBLING).astype(F32)
    chunk = half[:64]
    for k in (1, 2, 3):
        part = lax.ppermute(half[64 * k : 64 * k + 64].astype(BF), AXES, to_x(k))
        chunk = chunk + part.astype(F32)
    base = master - momentum_rate * momentum
    pieces = chunk[:, :2048].reshape(32, 16, 256).astype(BF)
    bases = jnp.broadcast_to(base.reshape(1, 16, 256).astype(BF), (32, 16, 256))
    extras = jnp.pad(chunk[:, 2048:].reshape(32, 2, 128), ((0, 0), (0, 14), (0, 0))).astype(BF)
    got = lax.all_to_all(jnp.concatenate([pieces, bases, extras], axis=2), YZ, 0, 0, tiled=True)
    weight_grad = jnp.sum(got[:, :, :256].astype(F32), axis=0).reshape(2, 2048)
    bn_grad = jnp.sum(got[:, :2, 512:520].astype(F32), axis=0)
    base_chunk = got[:, :, 256:512].reshape(64, 2048)
    step = weight_grad + decay_rate * master
    bn_step = bn_grad + decay_rate * own_bn
    bn_base = own_bn - momentum_rate * bn_momentum
    squares = jnp.stack(
        [
            jnp.stack([jnp.sum(weight_grad * weight_grad), jnp.sum(master * master)]),
            jnp.zeros((2,), F32),
        ]
    )
    squares = jnp.concatenate([squares, jnp.sum(bn_grad * bn_grad, 1)[:, None], jnp.sum(own_bn * own_bn, 1)[:, None]], axis=1)
    own_extra = jnp.concatenate([*hi_lo(bn_step), *hi_lo(bn_base), *hi_lo(squares)], axis=1)
    own_piece = jnp.concatenate([step.reshape(16, 256).astype(BF), jnp.pad(own_extra, ((0, 14), (0, 88)))], axis=1)
    got = lax.all_to_all(jnp.broadcast_to(own_piece[None], (32, 16, 384)), YZ, 0, 0, tiled=True)
    chunk = jnp.concatenate([got[:, :, :256].reshape(64, 2048), got[:, :2, 256:].reshape(64, 128)], axis=1)

    def spread(block):
        parts = [block] + [lax.ppermute(block, AXES, to_x(-k % 4)) for k in (1, 2, 3)]
        mine_half = jnp.concatenate(parts, axis=0)
        other = lax.ppermute(mine_half, AXES, SIBLING)
        return jnp.concatenate([mine_half, other], axis=0)

    base_all = spread(base_chunk)
    step_all = spread(chunk)
    tail = jnp.dot(sel, step_all[:, 2048:], preferred_element_type=F32)
    sq = jnp.sum((tail[:, 32:36] + tail[:, 36:40]).reshape(256, 2, 4), axis=0)
    g_sq = jnp.concatenate([sq[:1, 0], sq[:, 2]])
    w_sq = jnp.concatenate([sq[:1, 1], sq[:, 3]])
    w_norm = jnp.sqrt(w_sq)
    trust = trust_coef * w_norm / (jnp.sqrt(g_sq) + decay_rate * w_norm)
    rate = learn_rate * trust
    moved = (base_all.astype(F32) - rate[0] * step_all[:, :2048].astype(F32)).astype(BF)
    new_weight = jnp.dot(sel, moved, preferred_element_type=F32).astype(BF)
    tail = tail.reshape(256, 2, 128)
    bn_all = (tail[:, :, 16:24] + tail[:, :, 24:32]) - rate[1:][None, :, None] * (tail[:, :, 0:8] + tail[:, :, 8:16])
    new_bn = bn_all.transpose(1, 0, 2).reshape(2, 2048).astype(BF)
    new_momentum = momentum_rate * momentum + rate[0] * step
    new_master = master - new_momentum
    new_bn_momentum = momentum_rate * bn_momentum + rate[1:][:, None] * bn_step
    new_bn_master = own_bn - new_bn_momentum
    return (grad_input, up, new_master, new_momentum, new_weight, new_bn_master, new_bn_momentum, new_bn)


def solution(mesh):
    fine = Mesh(mesh.devices.reshape(SIZES), AXES)
    rows = P(AXES, None)
    cols = P(None, AXES)
    return jax.shard_map(
        shards,
        mesh=fine,
        in_specs=(rows, P(), rows, rows, P(), rows, rows, cols),
        out_specs=(rows, rows, rows, rows, P(), cols, cols, P()),
        check_vma=False,
    )
```

```python
import functools

import jax
import jax.numpy as jnp
from jax import lax
from jax.experimental import pallas as pl
from jax.experimental.pallas import tpu as pltpu
from jax.sharding import Mesh, PartitionSpec as P

eps_norm = 1e-05
momentum_rate = 0.9
learn_rate = 4.0
trust_coef = 0.001
decay_rate = 5e-05

AXES = ("zh", "x", "zl", "y", "c")
SIZES = (2, 4, 4, 4, 2)
GX = ("zh", "x")
XY = ("x", "y")
Z = ("zh", "zl")
BF = jnp.bfloat16
F32 = jnp.float32

ROWS = 392
CB = 512
C = 2048
EXT = 128
WIDE = C + EXT
PIECE = 2 * C + 2 * EXT
COLS = 512
STEPS = C // COLS
COUNT = float(ROWS * 8)
VMEM_BYTES = 24 * 1024 * 1024
VMEM_ALL = 60 * 1024 * 1024


def sibling_pairs():
    return [(i, i ^ 1) for i in range(256)]


def natural_row(t, c):
    cc = c ^ (t >> 8)
    return (
        ((t >> 3) & 1) * 256
        + ((t >> 6) & 3) * 64
        + ((t >> 1) & 3) * 16
        + ((t >> 4) & 3) * 4
        + cc * 2
        + (t & 1)
    )


def hi_lo(v):
    hi = v.astype(BF).astype(F32)
    return hi, v - hi


def params(limit=VMEM_BYTES):
    return pltpu.CompilerParams(vmem_limit_bytes=limit)


ANY = pl.BlockSpec(memory_space=pl.ANY)
VMEM = pl.BlockSpec(memory_space=pltpu.VMEM)
SMEM = pl.BlockSpec(memory_space=pltpu.SMEM)
DMA = pltpu.SemaphoreType.DMA


def copy(src, dst, sem):
    made = pltpu.make_async_copy(src, dst, sem)
    made.start()
    return made


def cols(j):
    return pl.ds(j * COLS, COLS)


def own_block(row, mine):
    block = jnp.zeros((2, EXT), F32)
    for q in range(16):
        block = jnp.where((mine >> 4) == q, row[:, EXT * q : EXT * q + EXT], block)
    return block


def stats_kernel(
    mine_ref, f_any, w_any, cot_any, pre_any, m_any, v_any, bn_any, bnm_any,
    up_any, stat_ref, base_ref,
    f, w, cot, pre, up, master, momentum, bn, bnm, sems,
):
    mine = mine_ref[0]
    first = copy(f_any, f, sems.at[0, STEPS])
    loads = []
    for j in range(STEPS):
        loads.append(
            [
                copy(w_any.at[:, cols(j)], w.at[:, cols(j)], sems.at[0, j]),
                copy(cot_any.at[:, cols(j)], cot.at[:, cols(j)], sems.at[1, j]),
                copy(pre_any.at[:, cols(j)], pre.at[:, cols(j)], sems.at[2, j]),
            ]
        )
    small = [
        copy(m_any, master, sems.at[1, STEPS]),
        copy(v_any, momentum, sems.at[2, STEPS]),
        copy(bn_any, bn, sems.at[3, STEPS]),
        copy(bnm_any, bnm, sems.at[4, 0]),
    ]
    first.wait()
    stores = []
    for j in range(STEPS):
        loads[j][0].wait()
        conv = jnp.dot(f[...], w[:, cols(j)], preferred_element_type=F32)
        loads[j][1].wait()
        loads[j][2].wait()
        u = jnp.where(pre[:, cols(j)].astype(F32) > 0, cot[:, cols(j)].astype(F32), 0.0)
        up[:, cols(j)] = u.astype(BF)
        stores.append(copy(up.at[:, cols(j)], up_any.at[:, cols(j)], sems.at[3, j]))
        stat = jnp.concatenate(
            [
                jnp.sum(conv, axis=0, keepdims=True),
                jnp.sum(conv * conv, axis=0, keepdims=True),
                jnp.sum(u, axis=0, keepdims=True),
                jnp.sum(u * conv, axis=0, keepdims=True),
            ],
            axis=0,
        )
        stat_ref[:, :, cols(j)] = jnp.broadcast_to(stat[None], (8, 4, COLS))
    for load in small:
        load.wait()
    base_ref[:, 0:C] = master[...] - momentum_rate * momentum[...]
    base_ref[:, C : 2 * C] = master[...]
    own_bn = own_block(bn[...], mine)
    lane = lax.broadcasted_iota(jnp.int32, (2, EXT), 1)
    bn_base = own_bn - momentum_rate * jnp.concatenate([bnm[...]] * 16, axis=1)
    base_ref[:, 2 * C : 2 * C + EXT] = jnp.where((lane >> 3) == (mine & 15), bn_base, 0.0)
    square = jnp.sum(master[...] * master[...], axis=(0, 1), keepdims=True)
    row = lax.broadcasted_iota(jnp.int32, (2, EXT), 0)
    base_ref[:, 2 * C + EXT :] = jnp.where((row == 0) & (lane == 0), square, 0.0)
    for store in stores:
        store.wait()


def stats_call(mine, features, weight, cotangent, pre_act, master, momentum, bn_params, bn_momentum):
    return pl.pallas_call(
        stats_kernel,
        in_specs=[SMEM] + [ANY] * 8,
        out_specs=[ANY, VMEM, VMEM],
        out_shape=[
            jax.ShapeDtypeStruct((ROWS, C), BF),
            jax.ShapeDtypeStruct((8, 4, C), F32),
            jax.ShapeDtypeStruct((2, PIECE), F32),
        ],
        scratch_shapes=[
            pltpu.VMEM((ROWS, CB), BF),
            pltpu.VMEM((CB, C), BF),
            pltpu.VMEM((ROWS, C), BF),
            pltpu.VMEM((ROWS, C), BF),
            pltpu.VMEM((ROWS, C), BF),
            pltpu.VMEM((2, C), F32),
            pltpu.VMEM((2, C), F32),
            pltpu.VMEM((2, C), F32),
            pltpu.VMEM((2, 8), F32),
            DMA((5, STEPS + 1)),
        ],
        compiler_params=params(VMEM_ALL),
        cost_estimate=pl.CostEstimate(flops=2 * ROWS * CB * C, bytes_accessed=7500000, transcendentals=0),
        name="stats",
    )(mine, features, weight, cotangent, pre_act, master, momentum, bn_params, bn_momentum)


def grad_kernel(
    c_ref, stat_any, f_any, w_any, up_any, bn_any, p1, p2, p3, p4, p5, p6, p7,
    gc_any, send_any, own_any, own_ext_ref,
    stat, bn, f, w, up, gc, send, own, ft, ext_send, ext_own, sems,
):
    c = c_ref[0]
    early = [copy(stat_any, stat, sems.at[3, STEPS]), copy(bn_any, bn, sems.at[4, STEPS])]
    first = copy(f_any, f, sems.at[0, STEPS])
    loads = []
    for j in range(STEPS):
        loads.append(
            [
                copy(w_any.at[:, cols(j)], w.at[:, cols(j)], sems.at[0, j]),
                copy(up_any.at[:, cols(j)], up.at[:, cols(j)], sems.at[1, j]),
            ]
        )
    t = lax.broadcasted_iota(jnp.int32, (CB, CB), 0)
    r = lax.broadcasted_iota(jnp.int32, (CB, CB), 1)
    sel = jnp.where(r == natural_row(t, c), 1.0, 0.0).astype(BF)
    for load in early:
        load.wait()
    sums = jnp.sum(stat[...], axis=0)
    mean = sums[0:1] / COUNT
    inv_std = lax.rsqrt(sums[1:2] / COUNT - mean * mean + eps_norm)
    sum_b = sums[2:3]
    sum_g = inv_std * (sums[3:4] - mean * sum_b)
    alpha = bn[0:1] * inv_std
    slope = alpha * inv_std * (sum_g / COUNT)
    shift = sum_b / COUNT
    scale_row = sum_g * 0.125
    shift_row = sum_b * 0.125
    mine = jnp.where(c == 0, scale_row, shift_row)
    other = jnp.where(c == 0, shift_row, scale_row)
    ext_send[...] = jnp.zeros_like(ext_send)
    ext_own[...] = jnp.zeros_like(ext_own)
    for q in range(16):
        ext_own[16 * q : 16 * q + 1, :] = mine[:, 128 * q : 128 * q + 128]
        ext_send[16 * q : 16 * q + 1, :] = other[:, 128 * q : 128 * q + 128]
    own_ext_ref[...] = ext_own[...]
    send[:, C:] = ext_send[...].astype(BF)
    stores = [copy(send.at[:, pl.ds(C, EXT)], send_any.at[:, pl.ds(C, EXT)], sems.at[2, STEPS])]
    first.wait()
    ft[...] = lax.dot_general(sel, f[...], (((1,), (1,)), ((), ())), preferred_element_type=F32).astype(BF)
    for j in range(STEPS):
        at = slice(j * COLS, j * COLS + COLS)
        loads[j][0].wait()
        conv = jnp.dot(f[...], w[:, at], preferred_element_type=F32)
        loads[j][1].wait()
        grad = alpha[:, at] * (up[:, at].astype(F32) - shift[:, at]) - (conv - mean[:, at]) * slope[:, at]
        grad = grad.astype(BF)
        gc[:, at] = grad
        stores.append(copy(gc.at[:, cols(j)], gc_any.at[:, cols(j)], sems.at[3, j]))
        g = jnp.dot(ft[...], grad, preferred_element_type=F32)
        send[:, at] = g[CB // 2 :].astype(BF)
        stores.append(copy(send.at[:, cols(j)], send_any.at[:, cols(j)], sems.at[2, j]))
        own[:, at] = g[: CB // 2]
        stores.append(copy(own.at[:, cols(j)], own_any.at[:, cols(j)], sems.at[4, j]))
    for store in stores:
        store.wait()


def grad_call(c, stats, features, weight, up, bn_params, pieces):
    return pl.pallas_call(
        grad_kernel,
        in_specs=[SMEM] + [ANY] * 12,
        out_specs=[ANY, ANY, ANY, VMEM],
        out_shape=[
            jax.ShapeDtypeStruct((ROWS, C), BF),
            jax.ShapeDtypeStruct((CB // 2, WIDE), BF),
            jax.ShapeDtypeStruct((CB // 2, C), F32),
            jax.ShapeDtypeStruct((CB // 2, EXT), F32),
        ],
        scratch_shapes=[
            pltpu.VMEM((8, 4, C), F32),
            pltpu.VMEM((2, C), F32),
            pltpu.VMEM((ROWS, CB), BF),
            pltpu.VMEM((CB, C), BF),
            pltpu.VMEM((ROWS, C), BF),
            pltpu.VMEM((ROWS, C), BF),
            pltpu.VMEM((CB // 2, WIDE), BF),
            pltpu.VMEM((CB // 2, C), F32),
            pltpu.VMEM((CB, ROWS), BF),
            pltpu.VMEM((CB // 2, EXT), F32),
            pltpu.VMEM((CB // 2, EXT), F32),
            DMA((5, STEPS + 1)),
        ],
        compiler_params=params(VMEM_ALL),
        cost_estimate=pl.CostEstimate(flops=4 * ROWS * CB * C, bytes_accessed=9000000, transcendentals=0),
        name="grad",
    )(c, stats, features, weight, up, bn_params, *pieces)


def input_kernel(
    z_ref, gc_any, w_any, p0, p1, p2, p3, p4, p5, p6, p7, out_ref, base_ref, rows_ref, sq_ref,
    gc, w, parts, pieces, sems
):
    rows = [copy(p, parts.at[k], sems.at[2, k]) for k, p in enumerate((p0, p1, p2, p3, p4, p5, p6, p7))]
    loads = []
    for j in range(STEPS):
        loads.append(
            [
                copy(gc_any.at[:, cols(j)], gc.at[:, cols(j)], sems.at[0, j]),
                copy(w_any.at[:, cols(j)], w.at[:, cols(j)], sems.at[1, j]),
            ]
        )
    for load in rows:
        load.wait()
    for k in range(8):
        pieces[2 * k : 2 * k + 2, :] = parts[k]
    got = pltpu.roll(pieces[...], 2 * z_ref[0], 0)
    base_ref[:, :C] = got[:, :C].astype(BF)
    base_ref[:, C:] = got[:, 2 * C : 2 * C + EXT].astype(BF)
    rows_ref[...] = got[:, C : 2 * C]
    sq_ref[...] = jnp.sum(got[:, 2 * C + EXT :], axis=(0, 1), keepdims=True)
    total = None
    for j in range(STEPS):
        loads[j][0].wait()
        loads[j][1].wait()
        part = lax.dot_general(
            gc[:, cols(j)], w[:, cols(j)], (((1,), (1,)), ((), ())), preferred_element_type=F32
        )
        total = part if total is None else total + part
    out_ref[...] = total.astype(BF)


def input_call(z, gc, weight, pieces):
    return pl.pallas_call(
        input_kernel,
        in_specs=[SMEM] + [ANY] * 10,
        out_specs=[VMEM] * 4,
        out_shape=[
            jax.ShapeDtypeStruct((ROWS, CB), BF),
            jax.ShapeDtypeStruct((16, WIDE), BF),
            jax.ShapeDtypeStruct((16, C), F32),
            jax.ShapeDtypeStruct((1, 1), F32),
        ],
        scratch_shapes=[
            pltpu.VMEM((ROWS, C), BF),
            pltpu.VMEM((CB, C), BF),
            pltpu.VMEM((8, 2, PIECE), F32),
            pltpu.VMEM((16, PIECE), F32),
            DMA((3, 8)),
        ],
        compiler_params=params(VMEM_ALL),
        cost_estimate=pl.CostEstimate(flops=2 * ROWS * CB * C, bytes_accessed=4000000, transcendentals=0),
        name="ginput",
    )(z, gc, weight, *pieces)


def pair_kernel(own_any, ext_ref, got_any, after_any, out_any, own, got, out, sems):
    rows = [pl.ds(64 * i, 64) for i in range(4)]
    loads = []
    for i in range(4):
        loads.append(
            [
                copy(own_any.at[rows[i]], own.at[rows[i]], sems.at[0, i]),
                copy(got_any.at[rows[i]], got.at[rows[i]], sems.at[1, i]),
            ]
        )
    stores = []
    for i in range(4):
        loads[i][0].wait()
        loads[i][1].wait()
        out[rows[i], :C] = (own[rows[i]] + got[rows[i], :C].astype(F32)).astype(BF)
        out[rows[i], C:] = (ext_ref[rows[i]] + got[rows[i], C:].astype(F32)).astype(BF)
        stores.append(copy(out.at[rows[i]], out_any.at[rows[i]], sems.at[2, i]))
    for store in stores:
        store.wait()


def pair_call(own, ext, got, after):
    return pl.pallas_call(
        pair_kernel,
        in_specs=[ANY, VMEM, ANY, ANY],
        out_specs=ANY,
        out_shape=jax.ShapeDtypeStruct((256, WIDE), BF),
        scratch_shapes=[
            pltpu.VMEM((256, C), F32),
            pltpu.VMEM((256, WIDE), BF),
            pltpu.VMEM((256, WIDE), BF),
            DMA((3, 4)),
        ],
        compiler_params=params(VMEM_ALL),
        cost_estimate=pl.CostEstimate(flops=256 * WIDE, bytes_accessed=4500000, transcendentals=0),
        name="pair",
    )(own, ext, got, after)


def plane_kernel(x_ref, got_any, b0, b1, b2, b3, out_any, base_any, got, out, sems):
    loads = [copy(got_any.at[pl.ds(4 * i, 4)], got.at[pl.ds(4 * i, 4)], sems.at[0, i]) for i in range(4)]
    stores = []
    for k, block in enumerate((b0, b1, b2, b3)):
        stores.append(copy(block, base_any.at[(x_ref[0] + k) & 3], sems.at[2, k]))
    total = None
    for i in range(4):
        loads[i].wait()
        part = jnp.sum(got[4 * i : 4 * i + 4].astype(F32), axis=0)
        total = part if total is None else total + part
    out[...] = total.astype(BF)
    stores += [copy(out, out_any.at[k], sems.at[1, k]) for k in range(8)]
    for store in stores:
        store.wait()


def plane_call(x, got, bases):
    return pl.pallas_call(
        plane_kernel,
        in_specs=[SMEM] + [ANY] * 5,
        out_specs=[ANY, ANY],
        out_shape=[jax.ShapeDtypeStruct((8, 16, WIDE), BF), jax.ShapeDtypeStruct((4, 16, WIDE), BF)],
        scratch_shapes=[pltpu.VMEM((16, 16, WIDE), BF), pltpu.VMEM((16, WIDE), BF), DMA((3, 8))],
        compiler_params=params(),
        cost_estimate=pl.CostEstimate(flops=256 * WIDE, bytes_accessed=1700000, transcendentals=0),
        name="plane",
    )(x, got, *bases)


def column_kernel(z_ref, got_ref, w_ref, sq_ref, b1, b2, b3, out_any, own_ref, send, sems):
    z = z_ref[0]
    total = jnp.sum(got_ref[...].astype(F32), axis=0)
    g = total[:, :C]
    w_hi, w_lo = hi_lo(sq_ref[...])
    g_hi, g_lo = hi_lo(jnp.sum(g * g, axis=(0, 1), keepdims=True))
    row = lax.broadcasted_iota(jnp.int32, (16, EXT), 0)
    lane = lax.broadcasted_iota(jnp.int32, (16, EXT), 1)
    bn_hi, bn_lo = hi_lo(total[0:1, C:])
    ext = jnp.where(row == 0, bn_hi, jnp.where(row == 1, bn_lo, 0.0))
    for k, value in enumerate((g_hi, g_lo, w_hi, w_lo)):
        ext = jnp.where((row == 2) & (lane == k), value, ext)
    send[:, :C] = (g + decay_rate * w_ref[...]).astype(BF)
    send[:, C:] = ext.astype(BF)
    stores = [copy(send, out_any.at[k], sems.at[k]) for k in range(16)]
    own_ref[...] = pltpu.roll(g, (16 - 2 * z) & 15, 0)[0:2]
    for store in stores:
        store.wait()


def column_call(z, got, w_rows, w_sq, bases):
    return pl.pallas_call(
        column_kernel,
        in_specs=[SMEM] + [VMEM] * 3 + [ANY] * 3,
        out_specs=[ANY, VMEM],
        out_shape=[
            jax.ShapeDtypeStruct((16, 16, WIDE), BF),
            jax.ShapeDtypeStruct((2, C), F32),
        ],
        scratch_shapes=[pltpu.VMEM((16, WIDE), BF), DMA((16,))],
        compiler_params=params(),
        cost_estimate=pl.CostEstimate(flops=128 * WIDE, bytes_accessed=1700000, transcendentals=0),
        name="column",
    )(z, got, w_rows, w_sq, *bases)


def basis_kernel(y_ref, b0, b1, b2, b3, after_any, base_any, sems):
    stores = []
    for k, block in enumerate((b0, b1, b2, b3)):
        for x in range(4):
            stores.append(copy(block.at[x], base_any.at[4 * x + ((y_ref[0] + k) & 3)], sems.at[4 * k + x]))
    for store in stores:
        store.wait()


def basis_call(y, bases, after):
    return pl.pallas_call(
        basis_kernel,
        in_specs=[SMEM] + [ANY] * 5,
        out_specs=ANY,
        out_shape=jax.ShapeDtypeStruct((16, 16, WIDE), BF),
        scratch_shapes=[DMA((16,))],
        compiler_params=params(),
        cost_estimate=pl.CostEstimate(flops=0, bytes_accessed=2200000, transcendentals=0),
        name="basis",
    )(y, *bases, after)


def update_kernel(
    at_ref, b0_any, b1_any, a0_any, a1_any, bn_any, g_any, m_any, v_any, bnm_any,
    nw_any, nbn_ref, nm_ref, nv_ref, nbm_ref, nbv_ref,
    b0, b1, a0, a1, nw, bn_v, g_v, m_v, v_v, bnm_v, sems,
):
    c = at_ref[0]
    mine = at_ref[1]
    last = pl.ds(C, EXT)
    main = pl.ds(0, C)
    big = ((b0_any, b0), (b1_any, b1), (a0_any, a0), (a1_any, a1))
    ends = [copy(src.at[:, last], dst.at[:, last], sems.at[4, k]) for k, (src, dst) in enumerate(big)]
    rows = [pl.ds(64 * i, 64) for i in range(4)]
    loads = []
    for i in range(4):
        loads.append(
            [copy(src.at[rows[i], main], dst.at[rows[i], main], sems.at[k, i]) for k, (src, dst) in enumerate(big)]
        )
    small = [
        copy(bn_any, bn_v, sems.at[7, 0]),
        copy(g_any, g_v, sems.at[7, 1]),
        copy(m_any, m_v, sems.at[7, 2]),
        copy(v_any, v_v, sems.at[7, 3]),
        copy(bnm_any, bnm_v, sems.at[8, 0]),
    ]
    r = lax.broadcasted_iota(jnp.int32, (128, 128), 0)
    t = lax.broadcasted_iota(jnp.int32, (128, 128), 1)
    want = (
        ((t >> 3) & 1) * 64 + ((t >> 1) & 3) * 16 + ((t >> 4) & 3) * 4 + (c ^ (t >> 6)) * 2 + (t & 1)
    )
    sel = jnp.where(r == want, 1.0, 0.0).astype(BF)

    for end in ends:
        end.wait()
    e0 = b0[:, C:].astype(F32)
    e1 = b1[:, C:].astype(F32)
    row = lax.broadcasted_iota(jnp.int32, (256, EXT), 0) & 15
    lane = lax.broadcasted_iota(jnp.int32, (256, EXT), 1)
    both = jnp.where(row == 2, e0 + e1, 0.0)
    g_sq = jnp.sum(jnp.where(lane < 2, both, 0.0), axis=(0, 1), keepdims=True)
    w_sq = jnp.sum(jnp.where((lane == 2) | (lane == 3), both, 0.0), axis=(0, 1), keepdims=True)

    def rate_of(w_sq, g_sq):
        w_norm = jnp.sqrt(w_sq)
        return learn_rate * (trust_coef * w_norm / (jnp.sqrt(g_sq) + decay_rate * w_norm))

    rate = rate_of(w_sq, g_sq)
    stores = []
    for i in range(4):
        for load in loads[i]:
            load.wait()
        at = slice(64 * i, 64 * i + 64)
        new = jnp.concatenate(
            [
                (a0[at, :C].astype(F32) - rate * b0[at, :C].astype(F32)).astype(BF),
                (a1[at, :C].astype(F32) - rate * b1[at, :C].astype(F32)).astype(BF),
            ],
            axis=0,
        )
        new = jnp.dot(sel, new, preferred_element_type=F32).astype(BF)
        nw[at, :] = new[:64]
        nw[slice(256 + 64 * i, 320 + 64 * i), :] = new[64:]
        stores.append(copy(nw.at[rows[i]], nw_any.at[rows[i]], sems.at[5, i]))
        far_rows = pl.ds(256 + 64 * i, 64)
        stores.append(copy(nw.at[far_rows], nw_any.at[far_rows], sems.at[6, i]))

    def flat(e):
        return jnp.concatenate([e[16 * q : 16 * q + 1] + e[16 * q + 1 : 16 * q + 2] for q in range(16)], axis=1)

    near, far = flat(e0), flat(e1)
    bn_grad = jnp.concatenate([jnp.where(c == 0, near, far), jnp.where(c == 0, far, near)], axis=0)
    for load in small:
        load.wait()
    bn = bn_v[...]
    bn_rate = rate_of(
        jnp.sum(bn * bn, axis=1, keepdims=True), jnp.sum(bn_grad * bn_grad, axis=1, keepdims=True)
    )
    ends_a = a0[:, C:].astype(F32) + a1[:, C:].astype(F32)
    blocks = [None] * 16
    for x in range(4):
        rows_x = ends_a[64 * x : 64 * x + 16]
        for y in range(1, 4):
            rows_x = rows_x + ends_a[64 * x + 16 * y : 64 * x + 16 * y + 16]
        for high in range(2):
            for half in range(2):
                top = 8 * high + 4 * half
                blocks[8 * high + 2 * x + half] = rows_x[top : top + 2] + rows_x[top + 2 : top + 4]
    bn_base = jnp.concatenate(blocks, axis=1)
    nbn_ref[...] = (bn_base - bn_rate * (bn_grad + decay_rate * bn)).astype(BF)
    master = m_v[...]
    new_v = momentum_rate * v_v[...] + rate * (g_v[...] + decay_rate * master)
    nv_ref[...] = new_v
    nm_ref[...] = master - new_v
    lane = lax.broadcasted_iota(jnp.int32, (2, EXT), 1)

    def own_eight(row):
        kept = jnp.where((lane >> 3) == (mine & 15), own_block(row, mine), 0.0)
        eight = kept[:, 0:8]
        for s in range(1, 16):
            eight = eight + kept[:, 8 * s : 8 * s + 8]
        return eight

    own_bn = own_eight(bn)
    new_bnv = momentum_rate * bnm_v[...] + bn_rate * (own_eight(bn_grad) + decay_rate * own_bn)
    nbv_ref[...] = new_bnv
    nbm_ref[...] = own_bn - new_bnv
    for store in stores:
        store.wait()


def update_call(at, b0, b1, a0, a1, bn_params, g_own, master, momentum, bn_momentum):
    small = [jax.ShapeDtypeStruct((2, C), F32)] * 2 + [jax.ShapeDtypeStruct((2, 8), F32)] * 2
    return pl.pallas_call(
        update_kernel,
        in_specs=[SMEM] + [ANY] * 4 + [ANY] * 5,
        out_specs=[ANY] + [VMEM] * 5,
        out_shape=[jax.ShapeDtypeStruct((CB, C), BF), jax.ShapeDtypeStruct((2, C), BF)] + small,
        scratch_shapes=[pltpu.VMEM((256, WIDE), BF)] * 4
        + [pltpu.VMEM((CB, C), BF)]
        + [pltpu.VMEM((2, C), F32)] * 4
        + [pltpu.VMEM((2, 8), F32), DMA((9, 4))],
        compiler_params=params(),
        cost_estimate=pl.CostEstimate(flops=2 * CB * 128 * C, bytes_accessed=6500000, transcendentals=0),
        name="update",
    )(at, b0, b1, a0, a1, bn_params, g_own, master, momentum, bn_momentum)


def exchange(block, axes):
    return lax.all_to_all(block, axes, 0, 0, tiled=True)


def shift_pairs(move):
    out = []
    for i in range(256):
        c, y, zl, x, zh = i & 1, (i >> 1) & 3, (i >> 3) & 3, (i >> 5) & 3, i >> 7
        x, y, z = move(x, y, 4 * zh + zl)
        out.append((i, ((((z >> 2) * 4 + x) * 4 + (z & 3)) * 4 + y) * 2 + c))
    return out


def ring(block, size, move):
    parts = [block]
    for k in range(1, size):
        parts.append(lax.ppermute(block, AXES, shift_pairs(functools.partial(move, size - k))))
    return parts


def number(*values):
    return jnp.stack(values).astype(jnp.int32)


def shards(features, weight, cotangent, pre_act, bn_params, master, momentum, bn_momentum):
    c, x, y, z = (lax.axis_index(axis) for axis in ("c", "x", "y", Z))
    mine = lax.axis_index(AXES)
    swap = functools.partial(lax.ppermute, axis_name=AXES, perm=sibling_pairs())

    up, stats, piece = stats_call(
        number(mine), features, weight, cotangent, pre_act, master, momentum, bn_params, bn_momentum
    )
    stats = exchange(stats, GX)
    pieces = ring(piece, 8, lambda k, x, y, z: (x, y, (z + k) % 8))
    gc, send, own, own_ext = grad_call(
        number(c), stats, features, weight, up, bn_params, pieces[1:]
    )
    grad_input, base, w_rows, w_sq = input_call(number(z), gc, weight, pieces)
    half = pair_call(own, own_ext, swap(send), grad_input)
    base, half = lax.optimization_barrier((base, half))
    bases = ring(base, 4, lambda k, x, y, z: ((x + k) % 4, y, z))
    part, base = plane_call(number(x), exchange(half.reshape(16, 16, WIDE), XY), bases)
    bases = ring(base, 4, lambda k, x, y, z: (x, (y + k) % 4, z))
    step, g_own = column_call(number(z), exchange(part, Z), w_rows, w_sq, bases[1:])
    a0 = basis_call(number(y), bases, step).reshape(256, WIDE)
    a1 = swap(a0)
    b0 = exchange(step, XY).reshape(256, WIDE)
    b1 = swap(b0)
    new_weight, new_bn, new_master, new_momentum, new_bn_master, new_bn_momentum = update_call(
        number(c, mine), b0, b1, a0, a1, bn_params, g_own, master, momentum, bn_momentum
    )
    return (grad_input, up, new_master, new_momentum, new_weight, new_bn_master, new_bn_momentum, new_bn)


def solution(mesh):
    fine = Mesh(mesh.devices.reshape(SIZES), AXES)
    rows = P(AXES, None)
    cols = P(None, AXES)
    return jax.shard_map(
        shards,
        mesh=fine,
        in_specs=(rows, P(), rows, rows, P(), rows, rows, cols),
        out_specs=(rows, rows, rows, rows, P(), cols, cols, P()),
        check_vma=False,
    )
```

```python
import functools

import jax
import jax.numpy as jnp
from jax import lax
from jax.experimental import pallas as pl
from jax.experimental.pallas import tpu as pltpu
from jax.sharding import Mesh, PartitionSpec as P

eps_norm = 1e-05
momentum_rate = 0.9
learn_rate = 4.0
trust_coef = 0.001
decay_rate = 5e-05

AXES = ("zh", "x", "zl", "y", "c")
SIZES = (2, 4, 4, 4, 2)
GX = ("zh", "x")
XY = ("x", "y")
Z = ("zh", "zl")
BF = jnp.bfloat16
F32 = jnp.float32

ROWS = 392
CB = 512
C = 2048
EXT = 128
WIDE = C + EXT
PIECE = 2 * C + 2 * EXT
COLS = 512
STEPS = C // COLS
COUNT = float(ROWS * 8)
VMEM_BYTES = 24 * 1024 * 1024
VMEM_ALL = 60 * 1024 * 1024


def sibling_pairs():
    return [(i, i ^ 1) for i in range(256)]


def natural_row(t, c):
    cc = c ^ (t >> 8)
    return (
        ((t >> 3) & 1) * 256
        + ((t >> 6) & 3) * 64
        + ((t >> 1) & 3) * 16
        + ((t >> 4) & 3) * 4
        + cc * 2
        + (t & 1)
    )


def hi_lo(v):
    hi = v.astype(BF).astype(F32)
    return hi, v - hi


def params(limit=VMEM_BYTES):
    return pltpu.CompilerParams(vmem_limit_bytes=limit)


ANY = pl.BlockSpec(memory_space=pl.ANY)
VMEM = pl.BlockSpec(memory_space=pltpu.VMEM)
SMEM = pl.BlockSpec(memory_space=pltpu.SMEM)
DMA = pltpu.SemaphoreType.DMA


TOKEN = jax.ShapeDtypeStruct((1, EXT), F32)


def done(token_ref):
    token_ref[...] = jnp.zeros_like(token_ref)


def copy(src, dst, sem):
    made = pltpu.make_async_copy(src, dst, sem)
    made.start()
    return made


def cols(j):
    return pl.ds(j * COLS, COLS)


def own_block(row, mine):
    block = jnp.zeros((2, EXT), F32)
    for q in range(16):
        block = jnp.where((mine >> 4) == q, row[:, EXT * q : EXT * q + EXT], block)
    return block


def stats_kernel(
    mine_ref, f_any, w_any, cot_any, pre_any, m_any, v_any, bn_any, bnm_any,
    stat_ref, base_ref,
    f, w, cot, pre, master, momentum, bn, bnm, sems,
):
    mine = mine_ref[0]
    first = copy(f_any, f, sems.at[0, STEPS])
    loads = []
    for j in range(STEPS):
        loads.append(
            [
                copy(w_any.at[:, cols(j)], w.at[:, cols(j)], sems.at[0, j]),
                copy(cot_any.at[:, cols(j)], cot.at[:, cols(j)], sems.at[1, j]),
                copy(pre_any.at[:, cols(j)], pre.at[:, cols(j)], sems.at[2, j]),
            ]
        )
    small = [
        copy(m_any, master, sems.at[1, STEPS]),
        copy(v_any, momentum, sems.at[2, STEPS]),
        copy(bn_any, bn, sems.at[3, STEPS]),
        copy(bnm_any, bnm, sems.at[4, 0]),
    ]
    first.wait()
    for j in range(STEPS):
        loads[j][0].wait()
        conv = jnp.dot(f[...], w[:, cols(j)], preferred_element_type=F32)
        loads[j][1].wait()
        loads[j][2].wait()
        u = jnp.where(pre[:, cols(j)].astype(F32) > 0, cot[:, cols(j)].astype(F32), 0.0)
        stat = jnp.concatenate(
            [
                jnp.sum(conv, axis=0, keepdims=True),
                jnp.sum(conv * conv, axis=0, keepdims=True),
                jnp.sum(u, axis=0, keepdims=True),
                jnp.sum(u * conv, axis=0, keepdims=True),
            ],
            axis=0,
        )
        stat_ref[:, :, cols(j)] = jnp.broadcast_to(stat[None], (8, 4, COLS))
    for load in small:
        load.wait()
    base_ref[:, 0:C] = master[...] - momentum_rate * momentum[...]
    base_ref[:, C : 2 * C] = master[...]
    own_bn = own_block(bn[...], mine)
    lane = lax.broadcasted_iota(jnp.int32, (2, EXT), 1)
    bn_base = own_bn - momentum_rate * jnp.concatenate([bnm[...]] * 16, axis=1)
    base_ref[:, 2 * C : 2 * C + EXT] = jnp.where((lane >> 3) == (mine & 15), bn_base, 0.0)
    square = jnp.sum(master[...] * master[...], axis=(0, 1), keepdims=True)
    row = lax.broadcasted_iota(jnp.int32, (2, EXT), 0)
    base_ref[:, 2 * C + EXT :] = jnp.where((row == 0) & (lane == 0), square, 0.0)


def stats_call(mine, features, weight, cotangent, pre_act, master, momentum, bn_params, bn_momentum):
    return pl.pallas_call(
        stats_kernel,
        in_specs=[SMEM] + [ANY] * 8,
        out_specs=[VMEM, VMEM],
        out_shape=[
            jax.ShapeDtypeStruct((8, 4, C), F32),
            jax.ShapeDtypeStruct((2, PIECE), F32),
        ],
        scratch_shapes=[
            pltpu.VMEM((ROWS, CB), BF),
            pltpu.VMEM((CB, C), BF),
            pltpu.VMEM((ROWS, C), BF),
            pltpu.VMEM((ROWS, C), BF),
            pltpu.VMEM((2, C), F32),
            pltpu.VMEM((2, C), F32),
            pltpu.VMEM((2, C), F32),
            pltpu.VMEM((2, 8), F32),
            DMA((5, STEPS + 1)),
        ],
        compiler_params=params(VMEM_ALL),
        cost_estimate=pl.CostEstimate(flops=2 * ROWS * CB * C, bytes_accessed=7500000, transcendentals=0),
        name="stats",
    )(mine, features, weight, cotangent, pre_act, master, momentum, bn_params, bn_momentum)


def prep_kernel(
    c_ref, f_any, w_any, cot_any, pre_any, up_any, conv_any, ft_ref, f, w, cot, pre, up, conv, sems
):
    first = copy(f_any, f, sems.at[0, STEPS])
    loads = []
    for j in range(STEPS):
        loads.append(
            [
                copy(w_any.at[:, cols(j)], w.at[:, cols(j)], sems.at[0, j]),
                copy(cot_any.at[:, cols(j)], cot.at[:, cols(j)], sems.at[1, j]),
                copy(pre_any.at[:, cols(j)], pre.at[:, cols(j)], sems.at[2, j]),
            ]
        )
    t = lax.broadcasted_iota(jnp.int32, (CB, CB), 0)
    r = lax.broadcasted_iota(jnp.int32, (CB, CB), 1)
    sel = jnp.where(r == natural_row(t, c_ref[0]), 1.0, 0.0).astype(BF)
    first.wait()
    ft_ref[...] = lax.dot_general(sel, f[...], (((1,), (1,)), ((), ())), preferred_element_type=F32).astype(BF)
    stores = []
    for j in range(STEPS):
        loads[j][0].wait()
        conv[:, cols(j)] = jnp.dot(f[...], w[:, cols(j)], preferred_element_type=F32)
        stores.append(copy(conv.at[:, cols(j)], conv_any.at[:, cols(j)], sems.at[4, j]))
        loads[j][1].wait()
        loads[j][2].wait()
        u = jnp.where(pre[:, cols(j)].astype(F32) > 0, cot[:, cols(j)].astype(F32), 0.0)
        up[:, cols(j)] = u.astype(BF)
        stores.append(copy(up.at[:, cols(j)], up_any.at[:, cols(j)], sems.at[3, j]))
    for store in stores:
        store.wait()


def prep_call(c, features, weight, cotangent, pre_act):
    return pl.pallas_call(
        prep_kernel,
        in_specs=[SMEM] + [ANY] * 4,
        out_specs=[ANY, ANY, VMEM],
        out_shape=[
            jax.ShapeDtypeStruct((ROWS, C), BF),
            jax.ShapeDtypeStruct((ROWS, C), F32),
            jax.ShapeDtypeStruct((CB, ROWS), BF),
        ],
        scratch_shapes=[
            pltpu.VMEM((ROWS, CB), BF),
            pltpu.VMEM((CB, C), BF),
            pltpu.VMEM((ROWS, C), BF),
            pltpu.VMEM((ROWS, C), BF),
            pltpu.VMEM((ROWS, C), BF),
            pltpu.VMEM((ROWS, C), F32),
            DMA((5, STEPS + 1)),
        ],
        compiler_params=params(VMEM_ALL),
        cost_estimate=pl.CostEstimate(flops=3 * ROWS * CB * C, bytes_accessed=7500000, transcendentals=0),
        name="prep",
    )(c, features, weight, cotangent, pre_act)


def grad_kernel(
    at_ref, stat_ref, up_any, conv_any, ft_ref, bn_any, p0, p1, p2, p3,
    gc_any, send_ref, own_ref, own_ext_ref, rows_ref,
    up, conv, gc, bn, ext_send, ext_own, rows, sems,
):
    c, zl = at_ref[0], at_ref[1]
    early = copy(bn_any, bn, sems.at[0, STEPS])
    loads = [
        [
            copy(conv_any.at[:, cols(j)], conv.at[:, cols(j)], sems.at[0, j]),
            copy(up_any.at[:, cols(j)], up.at[:, cols(j)], sems.at[1, j]),
        ]
        for j in range(STEPS)
    ]
    for k, piece in enumerate((p0, p1, p2, p3)):
        rows[2 * k : 2 * k + 2, :] = piece[...]
    rows_ref[...] = pltpu.roll(rows[...], 2 * zl, 0)
    sums = jnp.sum(stat_ref[...], axis=0)
    mean = sums[0:1] / COUNT
    inv_std = lax.rsqrt(sums[1:2] / COUNT - mean * mean + eps_norm)
    sum_b = sums[2:3]
    sum_g = inv_std * (sums[3:4] - mean * sum_b)
    early.wait()
    alpha = bn[0:1] * inv_std
    slope = alpha * inv_std * (sum_g / COUNT)
    shift = sum_b / COUNT
    scale_row = sum_g * 0.125
    shift_row = sum_b * 0.125
    mine = jnp.where(c == 0, scale_row, shift_row)
    other = jnp.where(c == 0, shift_row, scale_row)
    ext_send[...] = jnp.zeros_like(ext_send)
    ext_own[...] = jnp.zeros_like(ext_own)
    for q in range(16):
        ext_own[16 * q : 16 * q + 1, :] = mine[:, 128 * q : 128 * q + 128]
        ext_send[16 * q : 16 * q + 1, :] = other[:, 128 * q : 128 * q + 128]
    own_ext_ref[...] = ext_own[...]
    send_ref[:, C:] = ext_send[...].astype(BF)
    stores = []
    for j in range(STEPS):
        at = slice(j * COLS, j * COLS + COLS)
        for load in loads[j]:
            load.wait()
        grad = alpha[:, at] * (up[:, at].astype(F32) - shift[:, at])
        grad = (grad - (conv[:, at] - mean[:, at]) * slope[:, at]).astype(BF)
        gc[:, at] = grad
        stores.append(copy(gc.at[:, cols(j)], gc_any.at[:, cols(j)], sems.at[2, j]))
        g = jnp.dot(ft_ref[...], grad, preferred_element_type=F32)
        send_ref[:, at] = g[CB // 2 :].astype(BF)
        own_ref[:, at] = g[: CB // 2].astype(BF)
    for store in stores:
        store.wait()


def grad_call(at, stats, up, conv, ft, bn_params, pieces):
    return pl.pallas_call(
        grad_kernel,
        in_specs=[SMEM, VMEM, ANY, ANY, VMEM, ANY] + [VMEM] * 4,
        out_specs=[ANY] + [VMEM] * 4,
        out_shape=[
            jax.ShapeDtypeStruct((ROWS, C), BF),
            jax.ShapeDtypeStruct((CB // 2, WIDE), BF),
            jax.ShapeDtypeStruct((CB // 2, C), BF),
            jax.ShapeDtypeStruct((CB // 2, EXT), F32),
            jax.ShapeDtypeStruct((8, PIECE), F32),
        ],
        scratch_shapes=[
            pltpu.VMEM((ROWS, C), BF),
            pltpu.VMEM((ROWS, C), F32),
            pltpu.VMEM((ROWS, C), BF),
            pltpu.VMEM((2, C), F32),
            pltpu.VMEM((CB // 2, EXT), F32),
            pltpu.VMEM((CB // 2, EXT), F32),
            pltpu.VMEM((8, PIECE), F32),
            DMA((3, STEPS + 1)),
        ],
        compiler_params=params(VMEM_ALL),
        cost_estimate=pl.CostEstimate(flops=2 * ROWS * CB * C, bytes_accessed=9000000, transcendentals=0),
        name="grad",
    )(at, stats, up, conv, ft, bn_params, *pieces)


def input_kernel(gc_any, w_any, after_any, out_ref, token_ref, gc, w, sems):
    done(token_ref)
    loads = [
        [
            copy(gc_any.at[:, cols(j)], gc.at[:, cols(j)], sems.at[0, j]),
            copy(w_any.at[:, cols(j)], w.at[:, cols(j)], sems.at[1, j]),
        ]
        for j in range(STEPS)
    ]
    total = None
    for j in range(STEPS):
        for load in loads[j]:
            load.wait()
        part = lax.dot_general(
            gc[:, cols(j)], w[:, cols(j)], (((1,), (1,)), ((), ())), preferred_element_type=F32
        )
        total = part if total is None else total + part
    out_ref[...] = total.astype(BF)


def input_call(gc, weight, after):
    return pl.pallas_call(
        input_kernel,
        in_specs=[ANY, ANY, ANY],
        out_specs=[VMEM, VMEM],
        out_shape=[jax.ShapeDtypeStruct((ROWS, CB), BF), TOKEN],
        scratch_shapes=[pltpu.VMEM((ROWS, C), BF), pltpu.VMEM((CB, C), BF), DMA((2, STEPS))],
        compiler_params=params(VMEM_ALL),
        cost_estimate=pl.CostEstimate(flops=2 * ROWS * CB * C, bytes_accessed=4000000, transcendentals=0),
        name="ginput",
    )(gc, weight, after)


def rows_kernel(z_ref, near, far, after_any, base_ref, w_any, w, sem):
    first = z_ref[0] == 0
    low = jnp.where(first, near[...], far[...])
    high = jnp.where(first, far[...], near[...])
    both = jnp.concatenate([low, high], axis=0)
    w[:, :C] = both[:, C : 2 * C]
    w[:, C:] = both[:, 2 * C + EXT :]
    store = copy(w, w_any, sem)
    base_ref[:, :C] = both[:, :C].astype(BF)
    base_ref[:, C:] = both[:, 2 * C : 2 * C + EXT].astype(BF)
    store.wait()


def rows_call(zh, near, far, after):
    return pl.pallas_call(
        rows_kernel,
        in_specs=[SMEM, VMEM, VMEM, ANY],
        out_specs=[VMEM, ANY],
        out_shape=[jax.ShapeDtypeStruct((16, WIDE), BF), jax.ShapeDtypeStruct((16, WIDE), F32)],
        scratch_shapes=[pltpu.VMEM((16, WIDE), F32), DMA],
        compiler_params=params(),
        cost_estimate=pl.CostEstimate(flops=16 * PIECE, bytes_accessed=500000, transcendentals=0),
        name="rows",
    )(zh, near, far, after)


def pair_kernel(own_ref, ext_ref, got_ref, out_ref, token_ref):
    done(token_ref)
    out_ref[:, :C] = (own_ref[...].astype(F32) + got_ref[:, :C].astype(F32)).astype(BF)
    out_ref[:, C:] = (ext_ref[...] + got_ref[:, C:].astype(F32)).astype(BF)


def pair_call(own, ext, got):
    return pl.pallas_call(
        pair_kernel,
        in_specs=[VMEM] * 3,
        out_specs=[VMEM, VMEM],
        out_shape=[jax.ShapeDtypeStruct((256, WIDE), BF), TOKEN],
        compiler_params=params(),
        cost_estimate=pl.CostEstimate(flops=256 * WIDE, bytes_accessed=4500000, transcendentals=0),
        name="pair",
    )(own, ext, got)


def plane_kernel(x_ref, got_ref, b0, b1, b2, b3, out_ref, base_any, token_ref, sems):
    done(token_ref)
    stores = []
    for k, block in enumerate((b0, b1, b2, b3)):
        stores.append(copy(block, base_any.at[(x_ref[0] + k) & 3], sems.at[k]))
    total = jnp.sum(got_ref[...].astype(F32), axis=0).astype(BF)
    out_ref[...] = jnp.broadcast_to(total[None], out_ref.shape)
    for store in stores:
        store.wait()


def plane_call(x, got, bases):
    return pl.pallas_call(
        plane_kernel,
        in_specs=[SMEM, VMEM] + [ANY] * 4,
        out_specs=[VMEM, ANY, VMEM],
        out_shape=[
            jax.ShapeDtypeStruct((8, 16, WIDE), BF),
            jax.ShapeDtypeStruct((4, 16, WIDE), BF),
            TOKEN,
        ],
        scratch_shapes=[DMA((4,))],
        compiler_params=params(),
        cost_estimate=pl.CostEstimate(flops=256 * WIDE, bytes_accessed=1700000, transcendentals=0),
        name="plane",
    )(x, got, *bases)


def column_kernel(z_ref, got_ref, w_any, b1, b2, b3, after_any, out_ref, own_ref, token_ref, w, sem):
    done(token_ref)
    load = copy(w_any, w, sem)
    z = z_ref[0]
    total = jnp.sum(got_ref[...].astype(F32), axis=0)
    g = total[:, :C]
    g_hi, g_lo = hi_lo(jnp.sum(g * g, axis=(0, 1), keepdims=True))
    load.wait()
    w_hi, w_lo = hi_lo(jnp.sum(w[:, C:], axis=(0, 1), keepdims=True))
    row = lax.broadcasted_iota(jnp.int32, (16, EXT), 0)
    lane = lax.broadcasted_iota(jnp.int32, (16, EXT), 1)
    bn_hi, bn_lo = hi_lo(total[0:1, C:])
    ext = jnp.where(row == 0, bn_hi, jnp.where(row == 1, bn_lo, 0.0))
    for k, value in enumerate((g_hi, g_lo, w_hi, w_lo)):
        ext = jnp.where((row == 2) & (lane == k), value, ext)
    step = (g + decay_rate * w[:, :C]).astype(BF)
    out_ref[:, :, :C] = jnp.broadcast_to(step[None], (16, 16, C))
    out_ref[:, :, C:] = jnp.broadcast_to(ext.astype(BF)[None], (16, 16, EXT))
    own_ref[...] = pltpu.roll(g, (16 - 2 * z) & 15, 0)[0:2]


def column_call(z, got, w_rows, bases, after):
    return pl.pallas_call(
        column_kernel,
        in_specs=[SMEM, VMEM] + [ANY] * 5,
        out_specs=[VMEM] * 3,
        out_shape=[
            jax.ShapeDtypeStruct((16, 16, WIDE), BF),
            jax.ShapeDtypeStruct((2, C), F32),
            TOKEN,
        ],
        scratch_shapes=[pltpu.VMEM((16, WIDE), F32), DMA],
        compiler_params=params(),
        cost_estimate=pl.CostEstimate(flops=128 * WIDE, bytes_accessed=1700000, transcendentals=0),
        name="column",
    )(z, got, w_rows, *bases, after)


def basis_kernel(y_ref, b0, b1, b2, b3, m_any, v_any, bnm_any, after_any, base_any, keep_ref, bnm, sems):
    stores = [
        copy(m_any, keep_ref.at[:, pl.ds(0, C)], sems.at[16]),
        copy(v_any, keep_ref.at[:, pl.ds(C, C)], sems.at[17]),
    ]
    load = copy(bnm_any, bnm, sems.at[18])
    for k, block in enumerate((b0, b1, b2, b3)):
        for x in range(4):
            stores.append(copy(block.at[x], base_any.at[4 * x + ((y_ref[0] + k) & 3)], sems.at[4 * k + x]))
    load.wait()
    keep_ref[:, 2 * C :] = jnp.concatenate([bnm[...]] * 16, axis=1)
    for store in stores:
        store.wait()


def basis_call(y, bases, master, momentum, bn_momentum, after):
    return pl.pallas_call(
        basis_kernel,
        in_specs=[SMEM] + [ANY] * 8,
        out_specs=[ANY, VMEM],
        out_shape=[jax.ShapeDtypeStruct((16, 16, WIDE), BF), jax.ShapeDtypeStruct((2, 2 * C + EXT), F32)],
        scratch_shapes=[pltpu.VMEM((2, 8), F32), DMA((19,))],
        compiler_params=params(),
        cost_estimate=pl.CostEstimate(flops=0, bytes_accessed=2200000, transcendentals=0),
        name="basis",
    )(y, *bases, master, momentum, bn_momentum, after)


def update_kernel(
    at_ref, b0, b1, a0, a1, bn_v, g_v, keep,
    nw_any, nbn_ref, nm_ref, nv_ref, nbm_ref, nbv_ref,
    nw, sems,
):
    c = at_ref[0]
    mine = at_ref[1]
    rows = [pl.ds(64 * i, 64) for i in range(4)]
    r = lax.broadcasted_iota(jnp.int32, (128, 128), 0)
    t = lax.broadcasted_iota(jnp.int32, (128, 128), 1)
    want = (
        ((t >> 3) & 1) * 64 + ((t >> 1) & 3) * 16 + ((t >> 4) & 3) * 4 + (c ^ (t >> 6)) * 2 + (t & 1)
    )
    sel = jnp.where(r == want, 1.0, 0.0).astype(BF)

    e0 = b0[:, C:].astype(F32)
    e1 = b1[:, C:].astype(F32)
    row = lax.broadcasted_iota(jnp.int32, (256, EXT), 0) & 15
    lane = lax.broadcasted_iota(jnp.int32, (256, EXT), 1)
    both = jnp.where(row == 2, e0 + e1, 0.0)
    g_sq = jnp.sum(jnp.where(lane < 2, both, 0.0), axis=(0, 1), keepdims=True)
    w_sq = jnp.sum(jnp.where((lane == 2) | (lane == 3), both, 0.0), axis=(0, 1), keepdims=True)

    def rate_of(w_sq, g_sq):
        w_norm = jnp.sqrt(w_sq)
        return learn_rate * (trust_coef * w_norm / (jnp.sqrt(g_sq) + decay_rate * w_norm))

    rate = rate_of(w_sq, g_sq)
    stores = []
    for i in range(4):
        at = slice(64 * i, 64 * i + 64)
        new = jnp.concatenate(
            [
                (a0[at, :C].astype(F32) - rate * b0[at, :C].astype(F32)).astype(BF),
                (a1[at, :C].astype(F32) - rate * b1[at, :C].astype(F32)).astype(BF),
            ],
            axis=0,
        )
        new = jnp.dot(sel, new, preferred_element_type=F32).astype(BF)
        nw[at, :] = new[:64]
        nw[slice(256 + 64 * i, 320 + 64 * i), :] = new[64:]
        stores.append(copy(nw.at[rows[i]], nw_any.at[rows[i]], sems.at[0, i]))
        far_rows = pl.ds(256 + 64 * i, 64)
        stores.append(copy(nw.at[far_rows], nw_any.at[far_rows], sems.at[1, i]))

    def flat(e):
        return jnp.concatenate([e[16 * q : 16 * q + 1] + e[16 * q + 1 : 16 * q + 2] for q in range(16)], axis=1)

    near, far = flat(e0), flat(e1)
    bn_grad = jnp.concatenate([jnp.where(c == 0, near, far), jnp.where(c == 0, far, near)], axis=0)
    bn = bn_v[...]
    bn_rate = rate_of(
        jnp.sum(bn * bn, axis=1, keepdims=True), jnp.sum(bn_grad * bn_grad, axis=1, keepdims=True)
    )
    ends_a = a0[:, C:].astype(F32) + a1[:, C:].astype(F32)
    blocks = [None] * 16
    for x in range(4):
        rows_x = ends_a[64 * x : 64 * x + 16]
        for y in range(1, 4):
            rows_x = rows_x + ends_a[64 * x + 16 * y : 64 * x + 16 * y + 16]
        for high in range(2):
            for half in range(2):
                top = 8 * high + 4 * half
                blocks[8 * high + 2 * x + half] = rows_x[top : top + 2] + rows_x[top + 2 : top + 4]
    bn_base = jnp.concatenate(blocks, axis=1)
    nbn_ref[...] = (bn_base - bn_rate * (bn_grad + decay_rate * bn)).astype(BF)
    master = keep[:, 0:C]
    new_v = momentum_rate * keep[:, C : 2 * C] + rate * (g_v[...] + decay_rate * master)
    nv_ref[...] = new_v
    nm_ref[...] = master - new_v
    lane = lax.broadcasted_iota(jnp.int32, (2, EXT), 1)

    def own_eight(row):
        kept = jnp.where((lane >> 3) == (mine & 15), own_block(row, mine), 0.0)
        eight = kept[:, 0:8]
        for s in range(1, 16):
            eight = eight + kept[:, 8 * s : 8 * s + 8]
        return eight

    own_bn = own_eight(bn)
    new_bnv = momentum_rate * keep[:, 2 * C : 2 * C + 8] + bn_rate * (own_eight(bn_grad) + decay_rate * own_bn)
    nbv_ref[...] = new_bnv
    nbm_ref[...] = own_bn - new_bnv
    for store in stores:
        store.wait()


def update_call(at, b0, b1, a0, a1, bn_params, g_own, keep):
    small = [jax.ShapeDtypeStruct((2, C), F32)] * 2 + [jax.ShapeDtypeStruct((2, 8), F32)] * 2
    return pl.pallas_call(
        update_kernel,
        in_specs=[SMEM] + [VMEM] * 7,
        out_specs=[ANY] + [VMEM] * 5,
        out_shape=[jax.ShapeDtypeStruct((CB, C), BF), jax.ShapeDtypeStruct((2, C), BF)] + small,
        scratch_shapes=[pltpu.VMEM((CB, C), BF), DMA((2, 4))],
        compiler_params=params(),
        cost_estimate=pl.CostEstimate(flops=2 * CB * 128 * C, bytes_accessed=6500000, transcendentals=0),
        name="update",
    )(at, b0, b1, a0, a1, bn_params, g_own, keep)


def exchange(block, axes):
    return lax.all_to_all(block, axes, 0, 0, tiled=True)


def shift_pairs(move):
    out = []
    for i in range(256):
        c, y, zl, x, zh = i & 1, (i >> 1) & 3, (i >> 3) & 3, (i >> 5) & 3, i >> 7
        x, y, z = move(x, y, 4 * zh + zl)
        out.append((i, ((((z >> 2) * 4 + x) * 4 + (z & 3)) * 4 + y) * 2 + c))
    return out


def ring(block, size, move):
    parts = [block]
    for k in range(1, size):
        parts.append(lax.ppermute(block, AXES, shift_pairs(functools.partial(move, size - k))))
    return parts


def number(*values):
    return jnp.stack(values).astype(jnp.int32)


def shards(features, weight, cotangent, pre_act, bn_params, master, momentum, bn_momentum):
    c, x, y, z = (lax.axis_index(axis) for axis in ("c", "x", "y", Z))
    mine = lax.axis_index(AXES)
    swap = functools.partial(lax.ppermute, axis_name=AXES, perm=sibling_pairs())

    stats, piece = stats_call(
        number(mine), features, weight, cotangent, pre_act, master, momentum, bn_params, bn_momentum
    )
    pieces = ring(piece, 4, lambda k, x, y, z: (x, y, (z & 4) + ((z + k) & 3)))
    at, stats = lax.optimization_barrier((number(c, z & 3), stats))
    up, conv, ft = prep_call(at[:1], features, weight, cotangent, pre_act)
    stats = exchange(stats, GX)
    gc, send, own, own_ext, near = grad_call(at, stats, up, conv, ft, bn_params, pieces)
    far = lax.ppermute(near, AXES, shift_pairs(lambda x, y, z: (x, y, z ^ 4)))
    half, token = pair_call(own, own_ext, swap(send))
    base, w_rows = rows_call(number(z >> 2), near, far, token)
    bases = ring(base, 4, lambda k, x, y, z: ((x + k) % 4, y, z))
    part, base, token = plane_call(number(x), exchange(half.reshape(16, 16, WIDE), XY), bases)
    bases = ring(base, 4, lambda k, x, y, z: (x, (y + k) % 4, z))
    grad_input, token = input_call(gc, weight, token)
    step, g_own, token = column_call(number(z), exchange(part, Z), w_rows, bases[1:], token)
    a0, keep = basis_call(number(y), bases, master, momentum, bn_momentum, token)
    a0 = a0.reshape(256, WIDE)
    a1 = swap(a0)
    b0 = exchange(step, XY).reshape(256, WIDE)
    b1 = swap(b0)
    new_weight, new_bn, new_master, new_momentum, new_bn_master, new_bn_momentum = update_call(
        number(c, mine), b0, b1, a0, a1, bn_params, g_own, keep
    )
    return (grad_input, up, new_master, new_momentum, new_weight, new_bn_master, new_bn_momentum, new_bn)


def solution(mesh):
    fine = Mesh(mesh.devices.reshape(SIZES), AXES)
    rows = P(AXES, None)
    cols = P(None, AXES)
    return jax.shard_map(
        shards,
        mesh=fine,
        in_specs=(rows, P(), rows, rows, P(), rows, rows, cols),
        out_specs=(rows, rows, rows, rows, P(), cols, cols, P()),
        check_vma=False,
    )
```

```python
import functools

import jax
import jax.numpy as jnp
from jax import lax
from jax.experimental import pallas as pl
from jax.experimental.pallas import tpu as pltpu
from jax.sharding import Mesh, PartitionSpec as P

eps_norm = 1e-05
momentum_rate = 0.9
learn_rate = 4.0
trust_coef = 0.001
decay_rate = 5e-05

AXES = ("zh", "x", "zl", "y", "c")
SIZES = (2, 4, 4, 4, 2)
GX = ("zh", "x")
XY = ("x", "y")
Z = ("zh", "zl")
BF = jnp.bfloat16
F32 = jnp.float32

ROWS = 392
CB = 512
C = 2048
EXT = 128
WIDE = C + EXT
PIECE = 2 * C + 2 * EXT
COLS = 512
STEPS = C // COLS
STAT_COLS = 1024
STAT_STEPS = C // STAT_COLS
COUNT = float(ROWS * 8)
TALL = 400
KEPT = 2 * TALL + CB // 4
VMEM_BYTES = 24 * 1024 * 1024
VMEM_ALL = 60 * 1024 * 1024


def sibling_pairs():
    return [(i, i ^ 1) for i in range(256)]


def natural_row(t, c):
    cc = c ^ (t >> 8)
    return (
        ((t >> 3) & 1) * 256
        + ((t >> 6) & 3) * 64
        + ((t >> 1) & 3) * 16
        + ((t >> 4) & 3) * 4
        + cc * 2
        + (t & 1)
    )


def hi_lo(v):
    hi = v.astype(BF).astype(F32)
    return hi, v - hi


def params(limit=VMEM_BYTES):
    return pltpu.CompilerParams(vmem_limit_bytes=limit)


ANY = pl.BlockSpec(memory_space=pl.ANY)
VMEM = pl.BlockSpec(memory_space=pltpu.VMEM)
SMEM = pl.BlockSpec(memory_space=pltpu.SMEM)
DMA = pltpu.SemaphoreType.DMA


TOKEN = jax.ShapeDtypeStruct((1,), jnp.int32)


def done(token_ref):
    token_ref[0] = 0


def copy(src, dst, sem):
    made = pltpu.make_async_copy(src, dst, sem)
    made.start()
    return made


def cols(j):
    return pl.ds(j * COLS, COLS)


def stat_cols(j):
    return pl.ds(j * STAT_COLS, STAT_COLS)


def place():
    at = lax.axis_index("zh")
    for axis, size in zip(AXES[1:], SIZES[1:]):
        at = at * size + lax.axis_index(axis)
    return at


def own_block(row, mine):
    block = jnp.zeros((2, EXT), F32)
    for q in range(16):
        block = jnp.where((mine >> 4) == q, row[:, EXT * q : EXT * q + EXT], block)
    return block


def stats_kernel(
    f_any, w_any, cot_any, pre_any, m_any, v_any, bn_any, bnm_any,
    stat_ref, base_ref,
    f, w, cot, pre, master, momentum, bn, bnm, sems,
):
    mine = place()
    first = copy(f_any, f, sems.at[0, STAT_STEPS])
    loads = []
    for j in range(STAT_STEPS):
        loads.append(
            [
                copy(w_any.at[:, stat_cols(j)], w.at[:, stat_cols(j)], sems.at[0, j]),
                copy(cot_any.at[:, stat_cols(j)], cot.at[:, stat_cols(j)], sems.at[1, j]),
                copy(pre_any.at[:, stat_cols(j)], pre.at[:, stat_cols(j)], sems.at[2, j]),
            ]
        )
    small = [
        copy(m_any, master, sems.at[1, STAT_STEPS]),
        copy(v_any, momentum, sems.at[2, STAT_STEPS]),
        copy(bn_any, bn, sems.at[3, STAT_STEPS]),
        copy(bnm_any, bnm, sems.at[4, 0]),
    ]
    first.wait()
    for j in range(STAT_STEPS):
        loads[j][0].wait()
        conv = jnp.dot(f[...], w[:, stat_cols(j)], preferred_element_type=F32)
        loads[j][1].wait()
        loads[j][2].wait()
        u = jnp.where(pre[:, stat_cols(j)].astype(F32) > 0, cot[:, stat_cols(j)].astype(F32), 0.0)
        stat = jnp.concatenate(
            [
                jnp.sum(conv, axis=0, keepdims=True),
                jnp.sum(conv * conv, axis=0, keepdims=True),
                jnp.sum(u, axis=0, keepdims=True),
                jnp.sum(u * conv, axis=0, keepdims=True),
            ],
            axis=0,
        )
        stat_ref[:, :, stat_cols(j)] = jnp.broadcast_to(stat[None], (8, 4, STAT_COLS))
    for load in small:
        load.wait()
    base_ref[:, 0:C] = master[...] - momentum_rate * momentum[...]
    base_ref[:, C : 2 * C] = master[...]
    own_bn = own_block(bn[...], mine)
    lane = lax.broadcasted_iota(jnp.int32, (2, EXT), 1)
    bn_base = own_bn - momentum_rate * jnp.concatenate([bnm[...]] * 16, axis=1)
    base_ref[:, 2 * C : 2 * C + EXT] = jnp.where((lane >> 3) == (mine & 15), bn_base, 0.0)
    square = jnp.sum(master[...] * master[...], axis=(0, 1), keepdims=True)
    row = lax.broadcasted_iota(jnp.int32, (2, EXT), 0)
    hi, lo = hi_lo(square)
    square = jnp.where(lane == 0, hi, jnp.where(lane == 1, lo, 0.0))
    base_ref[:, 2 * C + EXT :] = jnp.where(row == 0, square, 0.0)


def stats_call(features, weight, cotangent, pre_act, master, momentum, bn_params, bn_momentum):
    return pl.pallas_call(
        stats_kernel,
        in_specs=[ANY] * 8,
        out_specs=[VMEM, VMEM],
        out_shape=[
            jax.ShapeDtypeStruct((8, 4, C), F32),
            jax.ShapeDtypeStruct((2, PIECE), F32),
        ],
        scratch_shapes=[
            pltpu.VMEM((ROWS, CB), BF),
            pltpu.VMEM((CB, C), BF),
            pltpu.VMEM((ROWS, C), BF),
            pltpu.VMEM((ROWS, C), BF),
            pltpu.VMEM((2, C), F32),
            pltpu.VMEM((2, C), F32),
            pltpu.VMEM((2, C), F32),
            pltpu.VMEM((2, 8), F32),
            DMA((5, STAT_STEPS + 1)),
        ],
        compiler_params=params(VMEM_ALL),
        cost_estimate=pl.CostEstimate(flops=2 * ROWS * CB * C, bytes_accessed=7500000, transcendentals=0),
        name="stats",
    )(features, weight, cotangent, pre_act, master, momentum, bn_params, bn_momentum)


def prep_kernel(
    f_any, w_any, cot_any, pre_any, up_any, kept_any, f, w, cot, pre, up, tall, mid, ft, sems
):
    first = copy(f_any, f, sems.at[5, 0])
    loads = [
        [
            copy(w_any.at[:, cols(j)], w.at[:, cols(j)], sems.at[0, j]),
            copy(cot_any.at[:, cols(j)], cot.at[:, cols(j)], sems.at[1, j]),
            copy(pre_any.at[:, cols(j)], pre.at[:, cols(j)], sems.at[2, j]),
        ]
        for j in range(STEPS)
    ]
    t = lax.broadcasted_iota(jnp.int32, (CB, CB), 0)
    r = lax.broadcasted_iota(jnp.int32, (CB, CB), 1)
    sel = jnp.where(r == natural_row(t, lax.axis_index("c")), 1.0, 0.0).astype(BF)
    first.wait()
    ft[...] = jnp.zeros_like(ft)
    got = lax.dot_general(sel, f[...], (((1,), (1,)), ((), ())), preferred_element_type=F32).astype(BF)
    for b in range(4):
        ft[:, CB * b : CB * b + ROWS] = got[128 * b : 128 * b + 128]
    blank = jnp.zeros((TALL - ROWS, COLS), F32)
    stores = [copy(ft, kept_any.at[pl.ds(2 * TALL, CB // 4)], sems.at[5, 1])]
    for j in range(STEPS):
        loads[j][0].wait()
        conv = jnp.dot(f[...], w[:, cols(j)], preferred_element_type=F32)
        centre = jnp.sum(conv, axis=0, keepdims=True) / ROWS
        mid[:, cols(j)] = jnp.concatenate([conv - centre, blank], axis=0).astype(BF)
        stores.append(copy(mid.at[:, cols(j)], kept_any.at[pl.ds(TALL, TALL), cols(j)], sems.at[4, j]))
        loads[j][1].wait()
        loads[j][2].wait()
        u = jnp.where(pre[:, cols(j)].astype(F32) > 0, cot[:, cols(j)].astype(F32), 0.0)
        up[:, cols(j)] = u.astype(BF)
        stores.append(copy(up.at[:, cols(j)], up_any.at[:, cols(j)], sems.at[3, j]))
        tall[:, cols(j)] = jnp.concatenate([u, blank], axis=0).astype(BF)
        stores.append(copy(tall.at[:, cols(j)], kept_any.at[pl.ds(0, TALL), cols(j)], sems.at[6, j]))
    for store in stores:
        store.wait()


def prep_call(features, weight, cotangent, pre_act):
    return pl.pallas_call(
        prep_kernel,
        in_specs=[ANY] * 4,
        out_specs=[ANY, ANY],
        out_shape=[
            jax.ShapeDtypeStruct((ROWS, C), BF),
            jax.ShapeDtypeStruct((KEPT, C), BF),
        ],
        scratch_shapes=[
            pltpu.VMEM((ROWS, CB), BF),
            pltpu.VMEM((CB, C), BF),
            pltpu.VMEM((ROWS, C), BF),
            pltpu.VMEM((ROWS, C), BF),
            pltpu.VMEM((ROWS, C), BF),
            pltpu.VMEM((TALL, C), BF),
            pltpu.VMEM((TALL, C), BF),
            pltpu.VMEM((CB // 4, C), BF),
            DMA((7, STEPS)),
        ],
        compiler_params=params(VMEM_ALL),
        cost_estimate=pl.CostEstimate(flops=3 * ROWS * CB * C, bytes_accessed=9000000, transcendentals=0),
        name="prep",
    )(features, weight, cotangent, pre_act)


def grad_of(up, mid, coef):
    return (coef[0:1] * (up.astype(F32) - coef[1:2]) - (mid.astype(F32) + coef[2:3]) * coef[3:4]).astype(BF)


def grad_kernel(
    stat, kept, bn, p0, p1, send, own, near_ref, coef_ref, ext_send, ext_own
):
    c, zh = lax.axis_index("c"), lax.axis_index("zh")
    up = kept.at[0:TALL]
    mid = kept.at[TALL : 2 * TALL]
    low = jnp.where(zh == 0, p0[...], p1[...])
    high = jnp.where(zh == 0, p1[...], p0[...])
    near_ref[...] = jnp.concatenate([low, high], axis=0).astype(BF)
    sums = jnp.sum(stat[...], axis=0)
    mean = sums[0:1] / COUNT
    inv_std = lax.rsqrt(sums[1:2] / COUNT - mean * mean + eps_norm)
    sum_b = sums[2:3]
    sum_g = inv_std * (sums[3:4] - mean * sum_b)
    alpha = bn[0:1] * inv_std
    slope = alpha * inv_std * (sum_g / COUNT)
    shift = sum_b / COUNT
    centre = stat[4 * zh + lax.axis_index("x")][0:1] / ROWS
    coef = jnp.concatenate([alpha, shift, centre - mean, slope], axis=0)
    coef_ref[...] = coef
    scale_row = sum_g * 0.125
    shift_row = sum_b * 0.125
    mine = jnp.where(c == 0, scale_row, shift_row)
    other = jnp.where(c == 0, shift_row, scale_row)
    ext_send[...] = jnp.zeros_like(ext_send)
    ext_own[...] = jnp.zeros_like(ext_own)
    for q in range(16):
        ext_own[16 * q : 16 * q + 1, :] = mine[:, 128 * q : 128 * q + 128]
        ext_send[16 * q : 16 * q + 1, :] = other[:, 128 * q : 128 * q + 128]
    own[:, C:] = ext_own[...].astype(BF)
    send[:, C:] = ext_send[...].astype(BF)
    ft = jnp.concatenate([kept[2 * TALL :, CB * b : CB * b + TALL] for b in range(4)], axis=0)
    for j in range(STEPS):
        at = slice(j * COLS, j * COLS + COLS)
        g = jnp.dot(ft, grad_of(up[:, at], mid[:, at], coef[:, at]), preferred_element_type=F32)
        send[:, at] = g[CB // 2 :].astype(BF)
        own[:, at] = g[: CB // 2].astype(BF)


def grad_call(stats, kept, bn_params, pieces):
    return pl.pallas_call(
        grad_kernel,
        in_specs=[VMEM] * 5,
        out_specs=[VMEM] * 4,
        out_shape=[
            jax.ShapeDtypeStruct((CB // 2, WIDE), BF),
            jax.ShapeDtypeStruct((CB // 2, WIDE), BF),
            jax.ShapeDtypeStruct((4, PIECE), BF),
            jax.ShapeDtypeStruct((4, C), F32),
        ],
        scratch_shapes=[
            pltpu.VMEM((CB // 2, EXT), F32),
            pltpu.VMEM((CB // 2, EXT), F32),
        ],
        compiler_params=params(),
        cost_estimate=pl.CostEstimate(flops=2 * ROWS * CB * C, bytes_accessed=7000000, transcendentals=0),
        name="grad",
    )(stats, kept, bn_params, *pieces)


def input_kernel(w_any, kept_any, coef_any, after_ref, out_ref, token_ref, w, up, mid, coef, sems):
    done(token_ref)
    early = copy(coef_any, coef, sems.at[3, 0])
    loads = [
        [
            copy(w_any.at[:, cols(j)], w.at[:, cols(j)], sems.at[0, j]),
            copy(kept_any.at[pl.ds(0, TALL), cols(j)], up.at[:, cols(j)], sems.at[1, j]),
            copy(kept_any.at[pl.ds(TALL, TALL), cols(j)], mid.at[:, cols(j)], sems.at[2, j]),
        ]
        for j in range(STEPS)
    ]
    early.wait()
    total = None
    for j in range(STEPS):
        for load in loads[j]:
            load.wait()
        part = lax.dot_general(
            grad_of(up[:, cols(j)], mid[:, cols(j)], coef[:, cols(j)]),
            w[:, cols(j)],
            (((1,), (1,)), ((), ())),
            preferred_element_type=F32,
        )
        total = part if total is None else total + part
    out_ref[...] = total[:ROWS].astype(BF)


def input_call(weight, kept, coef, after):
    return pl.pallas_call(
        input_kernel,
        in_specs=[ANY] * 3 + [SMEM],
        out_specs=[VMEM, SMEM],
        out_shape=[jax.ShapeDtypeStruct((ROWS, CB), BF), TOKEN],
        scratch_shapes=[
            pltpu.VMEM((CB, C), BF),
            pltpu.VMEM((TALL, C), BF),
            pltpu.VMEM((TALL, C), BF),
            pltpu.VMEM((4, C), F32),
            DMA((4, STEPS)),
        ],
        compiler_params=params(VMEM_ALL),
        cost_estimate=pl.CostEstimate(flops=2 * ROWS * CB * C, bytes_accessed=5500000, transcendentals=0),
        name="ginput",
    )(weight, kept, coef, after)


def rows_kernel(n0, n1, n2, n3, after_ref, base_ref, w_any, four, w, sem):
    zl = lax.axis_index("zl")
    halves = []
    for high in range(2):
        for k, block in enumerate((n0, n1, n2, n3)):
            four[2 * k : 2 * k + 2, :] = block[...].astype(F32)[2 * high : 2 * high + 2]
        halves.append(pltpu.roll(four[...], 2 * zl, 0))
    both = jnp.concatenate(halves, axis=0)
    w[:, :C] = both[:, C : 2 * C]
    w[:, C:] = both[:, 2 * C + EXT :]
    store = copy(w, w_any, sem)
    base_ref[:, :C] = both[:, :C].astype(BF)
    base_ref[:, C:] = both[:, 2 * C : 2 * C + EXT].astype(BF)
    store.wait()


def rows_call(blocks, after):
    return pl.pallas_call(
        rows_kernel,
        in_specs=[VMEM] * 4 + [SMEM],
        out_specs=[VMEM, ANY],
        out_shape=[jax.ShapeDtypeStruct((16, WIDE), BF), jax.ShapeDtypeStruct((16, WIDE), F32)],
        scratch_shapes=[pltpu.VMEM((8, PIECE), F32), pltpu.VMEM((16, WIDE), F32), DMA],
        compiler_params=params(),
        cost_estimate=pl.CostEstimate(flops=16 * PIECE, bytes_accessed=500000, transcendentals=0),
        name="rows",
    )(*blocks, after)


def pair_kernel(own_ref, got_ref, out_ref, token_ref):
    done(token_ref)
    out_ref[...] = (own_ref[...].astype(F32) + got_ref[...].astype(F32)).astype(BF)


def pair_call(own, got):
    return pl.pallas_call(
        pair_kernel,
        in_specs=[VMEM] * 2,
        out_specs=[VMEM, SMEM],
        out_shape=[jax.ShapeDtypeStruct((256, WIDE), BF), TOKEN],
        compiler_params=params(),
        cost_estimate=pl.CostEstimate(flops=256 * WIDE, bytes_accessed=3300000, transcendentals=0),
        name="pair",
    )(own, got)


def plane_kernel(got_ref, b0, b1, b2, b3, out_ref, base_any, token_ref, sems):
    done(token_ref)
    x = lax.axis_index("x")
    stores = []
    for k, block in enumerate((b0, b1, b2, b3)):
        stores.append(copy(block, base_any.at[(x + k) & 3], sems.at[k]))
    total = jnp.sum(got_ref[...].astype(F32), axis=0).astype(BF)
    out_ref[...] = jnp.broadcast_to(total[None], out_ref.shape)
    for store in stores:
        store.wait()


def plane_call(got, bases):
    return pl.pallas_call(
        plane_kernel,
        in_specs=[VMEM] + [ANY] * 4,
        out_specs=[VMEM, ANY, SMEM],
        out_shape=[
            jax.ShapeDtypeStruct((8, 16, WIDE), BF),
            jax.ShapeDtypeStruct((4, 16, WIDE), BF),
            TOKEN,
        ],
        scratch_shapes=[DMA((4,))],
        compiler_params=params(),
        cost_estimate=pl.CostEstimate(flops=256 * WIDE, bytes_accessed=1700000, transcendentals=0),
        name="plane",
    )(got, *bases)


def column_kernel(got_ref, w_any, b1, b2, b3, after_ref, out_ref, own_ref, token_ref, w, sem):
    done(token_ref)
    load = copy(w_any, w, sem)
    z = 4 * lax.axis_index("zh") + lax.axis_index("zl")
    total = jnp.sum(got_ref[...].astype(F32), axis=0)
    g = total[:, :C]
    g_hi, g_lo = hi_lo(jnp.sum(g * g, axis=(0, 1), keepdims=True))
    load.wait()
    w_hi, w_lo = hi_lo(jnp.sum(w[:, C:], axis=(0, 1), keepdims=True))
    row = lax.broadcasted_iota(jnp.int32, (16, EXT), 0)
    lane = lax.broadcasted_iota(jnp.int32, (16, EXT), 1)
    bn_hi, bn_lo = hi_lo(total[0:1, C:])
    ext = jnp.where(row == 0, bn_hi, jnp.where(row == 1, bn_lo, 0.0))
    for k, value in enumerate((g_hi, g_lo, w_hi, w_lo)):
        ext = jnp.where((row == 2) & (lane == k), value, ext)
    step = (g + decay_rate * w[:, :C]).astype(BF)
    out_ref[:, :, :C] = jnp.broadcast_to(step[None], (16, 16, C))
    out_ref[:, :, C:] = jnp.broadcast_to(ext.astype(BF)[None], (16, 16, EXT))
    own_ref[...] = pltpu.roll(g, (16 - 2 * z) & 15, 0)[0:2]


def column_call(got, w_rows, bases, after):
    return pl.pallas_call(
        column_kernel,
        in_specs=[VMEM] + [ANY] * 4 + [SMEM],
        out_specs=[VMEM, VMEM, SMEM],
        out_shape=[
            jax.ShapeDtypeStruct((16, 16, WIDE), BF),
            jax.ShapeDtypeStruct((2, C), F32),
            TOKEN,
        ],
        scratch_shapes=[pltpu.VMEM((16, WIDE), F32), DMA],
        compiler_params=params(),
        cost_estimate=pl.CostEstimate(flops=128 * WIDE, bytes_accessed=1700000, transcendentals=0),
        name="column",
    )(got, w_rows, *bases, after)


def basis_kernel(b0, b1, b2, b3, m_any, v_any, bnm_any, after_ref, base_any, keep_ref, bnm, sems):
    y = lax.axis_index("y")
    stores = [
        copy(m_any, keep_ref.at[:, pl.ds(0, C)], sems.at[16]),
        copy(v_any, keep_ref.at[:, pl.ds(C, C)], sems.at[17]),
    ]
    load = copy(bnm_any, bnm, sems.at[18])
    for k, block in enumerate((b0, b1, b2, b3)):
        for x in range(4):
            stores.append(copy(block.at[x], base_any.at[4 * x + ((y + k) & 3)], sems.at[4 * k + x]))
    load.wait()
    keep_ref[:, 2 * C :] = jnp.concatenate([bnm[...]] * 16, axis=1)
    for store in stores:
        store.wait()


def basis_call(bases, master, momentum, bn_momentum, after):
    return pl.pallas_call(
        basis_kernel,
        in_specs=[ANY] * 7 + [SMEM],
        out_specs=[ANY, VMEM],
        out_shape=[jax.ShapeDtypeStruct((16, 16, WIDE), BF), jax.ShapeDtypeStruct((2, 2 * C + EXT), F32)],
        scratch_shapes=[pltpu.VMEM((2, 8), F32), DMA((19,))],
        compiler_params=params(),
        cost_estimate=pl.CostEstimate(flops=0, bytes_accessed=2200000, transcendentals=0),
        name="basis",
    )(*bases, master, momentum, bn_momentum, after)


def update_kernel(
    b0, b1, a0, a1, bn_v, g_v, keep,
    nw_any, nbn_ref, nm_ref, nv_ref, nbm_ref, nbv_ref,
    nw, sems,
):
    c = lax.axis_index("c")
    mine = place()
    rows = [pl.ds(64 * i, 64) for i in range(4)]
    r = lax.broadcasted_iota(jnp.int32, (128, 128), 0)
    t = lax.broadcasted_iota(jnp.int32, (128, 128), 1)
    want = (
        ((t >> 3) & 1) * 64 + ((t >> 1) & 3) * 16 + ((t >> 4) & 3) * 4 + (c ^ (t >> 6)) * 2 + (t & 1)
    )
    sel = jnp.where(r == want, 1.0, 0.0).astype(BF)

    e0 = b0[:, C:].astype(F32)
    e1 = b1[:, C:].astype(F32)
    row = lax.broadcasted_iota(jnp.int32, (256, EXT), 0) & 15
    lane = lax.broadcasted_iota(jnp.int32, (256, EXT), 1)
    both = jnp.where(row == 2, e0 + e1, 0.0)
    g_sq = jnp.sum(jnp.where(lane < 2, both, 0.0), axis=(0, 1), keepdims=True)
    w_sq = jnp.sum(jnp.where((lane == 2) | (lane == 3), both, 0.0), axis=(0, 1), keepdims=True)

    def rate_of(w_sq, g_sq):
        w_norm = jnp.sqrt(w_sq)
        return learn_rate * (trust_coef * w_norm / (jnp.sqrt(g_sq) + decay_rate * w_norm))

    rate = rate_of(w_sq, g_sq)
    stores = []
    for i in range(4):
        at = slice(64 * i, 64 * i + 64)
        new = jnp.concatenate(
            [
                (a0[at, :C].astype(F32) - rate * b0[at, :C].astype(F32)).astype(BF),
                (a1[at, :C].astype(F32) - rate * b1[at, :C].astype(F32)).astype(BF),
            ],
            axis=0,
        )
        new = jnp.dot(sel, new, preferred_element_type=F32).astype(BF)
        nw[at, :] = new[:64]
        nw[slice(256 + 64 * i, 320 + 64 * i), :] = new[64:]
        stores.append(copy(nw.at[rows[i]], nw_any.at[rows[i]], sems.at[0, i]))
        far_rows = pl.ds(256 + 64 * i, 64)
        stores.append(copy(nw.at[far_rows], nw_any.at[far_rows], sems.at[1, i]))

    def flat(e):
        return jnp.concatenate([e[16 * q : 16 * q + 1] + e[16 * q + 1 : 16 * q + 2] for q in range(16)], axis=1)

    near, far = flat(e0), flat(e1)
    bn_grad = jnp.concatenate([jnp.where(c == 0, near, far), jnp.where(c == 0, far, near)], axis=0)
    bn = bn_v[...]
    bn_rate = rate_of(
        jnp.sum(bn * bn, axis=1, keepdims=True), jnp.sum(bn_grad * bn_grad, axis=1, keepdims=True)
    )
    ends_a = a0[:, C:].astype(F32) + a1[:, C:].astype(F32)
    blocks = [None] * 16
    for x in range(4):
        rows_x = ends_a[64 * x : 64 * x + 16]
        for y in range(1, 4):
            rows_x = rows_x + ends_a[64 * x + 16 * y : 64 * x + 16 * y + 16]
        for high in range(2):
            for half in range(2):
                top = 8 * high + 4 * half
                blocks[8 * high + 2 * x + half] = rows_x[top : top + 2] + rows_x[top + 2 : top + 4]
    bn_base = jnp.concatenate(blocks, axis=1)
    nbn_ref[...] = (bn_base - bn_rate * (bn_grad + decay_rate * bn)).astype(BF)
    master = keep[:, 0:C]
    new_v = momentum_rate * keep[:, C : 2 * C] + rate * (g_v[...] + decay_rate * master)
    nv_ref[...] = new_v
    nm_ref[...] = master - new_v
    lane = lax.broadcasted_iota(jnp.int32, (2, EXT), 1)

    def own_eight(row):
        kept = jnp.where((lane >> 3) == (mine & 15), own_block(row, mine), 0.0)
        eight = kept[:, 0:8]
        for s in range(1, 16):
            eight = eight + kept[:, 8 * s : 8 * s + 8]
        return eight

    own_bn = own_eight(bn)
    new_bnv = momentum_rate * keep[:, 2 * C : 2 * C + 8] + bn_rate * (own_eight(bn_grad) + decay_rate * own_bn)
    nbv_ref[...] = new_bnv
    nbm_ref[...] = own_bn - new_bnv
    for store in stores:
        store.wait()


def update_call(b0, b1, a0, a1, bn_params, g_own, keep):
    small = [jax.ShapeDtypeStruct((2, C), F32)] * 2 + [jax.ShapeDtypeStruct((2, 8), F32)] * 2
    return pl.pallas_call(
        update_kernel,
        in_specs=[VMEM] * 7,
        out_specs=[ANY] + [VMEM] * 5,
        out_shape=[jax.ShapeDtypeStruct((CB, C), BF), jax.ShapeDtypeStruct((2, C), BF)] + small,
        scratch_shapes=[pltpu.VMEM((CB, C), BF), DMA((2, 4))],
        compiler_params=params(),
        cost_estimate=pl.CostEstimate(flops=2 * CB * 128 * C, bytes_accessed=6500000, transcendentals=0),
        name="update",
    )(b0, b1, a0, a1, bn_params, g_own, keep)


def exchange(block, axes):
    return lax.all_to_all(block, axes, 0, 0, tiled=True)


def shift_pairs(move):
    out = []
    for i in range(256):
        c, y, zl, x, zh = i & 1, (i >> 1) & 3, (i >> 3) & 3, (i >> 5) & 3, i >> 7
        x, y, z = move(x, y, 4 * zh + zl)
        out.append((i, ((((z >> 2) * 4 + x) * 4 + (z & 3)) * 4 + y) * 2 + c))
    return out


def ring(block, size, move):
    parts = [block]
    for k in range(1, size):
        parts.append(lax.ppermute(block, AXES, shift_pairs(functools.partial(move, size - k))))
    return parts


def shards(features, weight, cotangent, pre_act, bn_params, master, momentum, bn_momentum):
    swap = functools.partial(lax.ppermute, axis_name=AXES, perm=sibling_pairs())

    stats, piece = stats_call(
        features, weight, cotangent, pre_act, master, momentum, bn_params, bn_momentum
    )
    pieces = [piece, lax.ppermute(piece, AXES, shift_pairs(lambda x, y, z: (x, y, z ^ 4)))]
    later, stats = lax.optimization_barrier((features, stats))
    up, kept = prep_call(later, weight, cotangent, pre_act)
    stats = exchange(stats, GX)
    send, own, near, coef = grad_call(stats, kept, bn_params, pieces)
    half, token = pair_call(own, swap(send))
    blocks = ring(near, 4, lambda k, x, y, z: (x, y, (z & 4) + ((z + k) & 3)))
    base, w_rows = rows_call(blocks, token)
    bases = ring(base, 4, lambda k, x, y, z: ((x + k) % 4, y, z))
    part, base, token = plane_call(exchange(half.reshape(16, 16, WIDE), XY), bases)
    bases = ring(base, 4, lambda k, x, y, z: (x, (y + k) % 4, z))
    grad_input, token = input_call(weight, kept, coef, token)
    step, g_own, token = column_call(exchange(part, Z), w_rows, bases[1:], token)
    a0, keep = basis_call(bases, master, momentum, bn_momentum, token)
    a0 = a0.reshape(256, WIDE)
    a1 = swap(a0)
    b0 = exchange(step, XY).reshape(256, WIDE)
    b1 = swap(b0)
    new_weight, new_bn, new_master, new_momentum, new_bn_master, new_bn_momentum = update_call(
        b0, b1, a0, a1, bn_params, g_own, keep
    )
    return (grad_input, up, new_master, new_momentum, new_weight, new_bn_master, new_bn_momentum, new_bn)


def solution(mesh):
    fine = Mesh(mesh.devices.reshape(SIZES), AXES)
    rows = P(AXES, None)
    cols = P(None, AXES)
    return jax.shard_map(
        shards,
        mesh=fine,
        in_specs=(rows, P(), rows, rows, P(), rows, rows, cols),
        out_specs=(rows, rows, rows, rows, P(), cols, cols, P()),
        check_vma=False,
    )
```

```python
import functools

import jax
import jax.numpy as jnp
from jax import lax
from jax.experimental import pallas as pl
from jax.experimental.pallas import tpu as pltpu
from jax.sharding import Mesh, PartitionSpec as P

eps_norm = 1e-05
momentum_rate = 0.9
learn_rate = 4.0
trust_coef = 0.001
decay_rate = 5e-05

AXES = ("zh", "x", "zl", "y", "c")
SIZES = (2, 4, 4, 4, 2)
GX = ("zh", "x")
XY = ("x", "y")
Z = ("zh", "zl")
BF = jnp.bfloat16
F32 = jnp.float32

ROWS = 392
CB = 512
C = 2048
EXT = 128
WIDE = C + EXT
PIECE = 2 * C + 2 * EXT
COLS = 512
STEPS = C // COLS
STAT_COLS = 1024
STAT_STEPS = C // STAT_COLS
COUNT = float(ROWS * 8)
TALL = 400
KEPT = 2 * TALL + CB // 4
VMEM_BYTES = 24 * 1024 * 1024
VMEM_ALL = 60 * 1024 * 1024


def sibling_pairs():
    return [(i, i ^ 1) for i in range(256)]


def natural_row(t, c):
    cc = c ^ (t >> 8)
    return (
        ((t >> 3) & 1) * 256
        + ((t >> 6) & 3) * 64
        + ((t >> 1) & 3) * 16
        + ((t >> 4) & 3) * 4
        + cc * 2
        + (t & 1)
    )


def hi_lo(v):
    hi = v.astype(BF).astype(F32)
    return hi, v - hi


def params(limit=VMEM_BYTES):
    return pltpu.CompilerParams(vmem_limit_bytes=limit)


ANY = pl.BlockSpec(memory_space=pl.ANY)
VMEM = pl.BlockSpec(memory_space=pltpu.VMEM)
SMEM = pl.BlockSpec(memory_space=pltpu.SMEM)
DMA = pltpu.SemaphoreType.DMA


TOKEN = jax.ShapeDtypeStruct((1,), jnp.int32)


def done(token_ref):
    token_ref[0] = 0


def copy(src, dst, sem):
    made = pltpu.make_async_copy(src, dst, sem)
    made.start()
    return made


def cols(j):
    return pl.ds(j * COLS, COLS)


def stat_cols(j):
    return pl.ds(j * STAT_COLS, STAT_COLS)


def place():
    at = lax.axis_index("zh")
    for axis, size in zip(AXES[1:], SIZES[1:]):
        at = at * size + lax.axis_index(axis)
    return at


def own_block(row, mine):
    block = jnp.zeros((2, EXT), F32)
    for q in range(16):
        block = jnp.where((mine >> 4) == q, row[:, EXT * q : EXT * q + EXT], block)
    return block


def kept_part(pre, cot):
    return jnp.where(pre > 0, cot, jnp.zeros_like(cot))


def stats_kernel(
    f_any, w_any, cot_any, pre_any, m_any, v_any, bn_any, bnm_any,
    stat_ref, base_ref,
    f, w, cot, pre, master, momentum, bn, bnm, sems,
):
    mine = place()
    small = [
        copy(m_any, master, sems.at[1, STAT_STEPS]),
        copy(v_any, momentum, sems.at[2, STAT_STEPS]),
        copy(bn_any, bn, sems.at[3, STAT_STEPS]),
        copy(bnm_any, bnm, sems.at[4, 0]),
    ]
    first = copy(f_any, f, sems.at[0, STAT_STEPS])
    loads = []
    for j in range(STAT_STEPS):
        loads.append(
            [
                copy(w_any.at[:, stat_cols(j)], w.at[:, stat_cols(j)], sems.at[0, j]),
                copy(cot_any.at[:, stat_cols(j)], cot.at[:, stat_cols(j)], sems.at[1, j]),
                copy(pre_any.at[:, stat_cols(j)], pre.at[:, stat_cols(j)], sems.at[2, j]),
            ]
        )
    for load in small:
        load.wait()
    base_ref[:, 0:C] = (master[...] - momentum_rate * momentum[...]).astype(BF)
    base_ref[:, C : 2 * C] = master[...].astype(BF)
    own_bn = own_block(bn[...], mine)
    lane = lax.broadcasted_iota(jnp.int32, (2, EXT), 1)
    bn_base = own_bn - momentum_rate * jnp.concatenate([bnm[...]] * 16, axis=1)
    base_ref[:, 2 * C : 2 * C + EXT] = jnp.where((lane >> 3) == (mine & 15), bn_base, 0.0).astype(BF)
    square = jnp.sum(master[...] * master[...], axis=(0, 1), keepdims=True)
    row = lax.broadcasted_iota(jnp.int32, (2, EXT), 0)
    hi, lo = hi_lo(square)
    square = jnp.where(lane == 0, hi, jnp.where(lane == 1, lo, 0.0))
    base_ref[:, 2 * C + EXT :] = jnp.where(row == 0, square, 0.0).astype(BF)
    first.wait()
    for j in range(STAT_STEPS):
        loads[j][0].wait()
        conv = jnp.dot(f[...], w[:, stat_cols(j)], preferred_element_type=F32)
        loads[j][1].wait()
        loads[j][2].wait()
        u = kept_part(pre[:, stat_cols(j)], cot[:, stat_cols(j)]).astype(F32)
        stat = jnp.concatenate(
            [
                jnp.sum(conv, axis=0, keepdims=True),
                jnp.sum(conv * conv, axis=0, keepdims=True),
                jnp.sum(u, axis=0, keepdims=True),
                jnp.sum(u * conv, axis=0, keepdims=True),
            ],
            axis=0,
        )
        stat_ref[:, :, stat_cols(j)] = jnp.broadcast_to(stat[None], (8, 4, STAT_COLS))


def stats_call(features, weight, cotangent, pre_act, master, momentum, bn_params, bn_momentum):
    return pl.pallas_call(
        stats_kernel,
        in_specs=[ANY] * 8,
        out_specs=[VMEM, VMEM],
        out_shape=[
            jax.ShapeDtypeStruct((8, 4, C), F32),
            jax.ShapeDtypeStruct((2, PIECE), BF),
        ],
        scratch_shapes=[
            pltpu.VMEM((ROWS, CB), BF),
            pltpu.VMEM((CB, C), BF),
            pltpu.VMEM((ROWS, C), BF),
            pltpu.VMEM((ROWS, C), BF),
            pltpu.VMEM((2, C), F32),
            pltpu.VMEM((2, C), F32),
            pltpu.VMEM((2, C), F32),
            pltpu.VMEM((2, 8), F32),
            DMA((5, STAT_STEPS + 1)),
        ],
        compiler_params=params(VMEM_ALL),
        cost_estimate=pl.CostEstimate(flops=2 * ROWS * CB * C, bytes_accessed=7500000, transcendentals=0),
        name="stats",
    )(features, weight, cotangent, pre_act, master, momentum, bn_params, bn_momentum)


def prep_kernel(
    f_any, w_any, cot_any, pre_any, up_any, kept_any, f, w, cot, pre, up, tall, mid, ft, sems
):
    first = copy(f_any, f, sems.at[5, 0])
    loads = [
        [
            copy(w_any.at[:, cols(j)], w.at[:, cols(j)], sems.at[0, j]),
            copy(cot_any.at[:, cols(j)], cot.at[:, cols(j)], sems.at[1, j]),
            copy(pre_any.at[:, cols(j)], pre.at[:, cols(j)], sems.at[2, j]),
        ]
        for j in range(STEPS)
    ]
    t = lax.broadcasted_iota(jnp.int32, (CB, CB), 0)
    r = lax.broadcasted_iota(jnp.int32, (CB, CB), 1)
    sel = jnp.where(r == natural_row(t, lax.axis_index("c")), 1.0, 0.0).astype(BF)
    first.wait()
    ft[...] = jnp.zeros_like(ft)
    got = lax.dot_general(sel, f[...], (((1,), (1,)), ((), ())), preferred_element_type=F32).astype(BF)
    for b in range(4):
        ft[:, CB * b : CB * b + ROWS] = got[128 * b : 128 * b + 128]
    blank = jnp.zeros((TALL - ROWS, COLS), F32)
    stores = [copy(ft, kept_any.at[pl.ds(2 * TALL, CB // 4)], sems.at[5, 1])]
    for j in range(STEPS):
        loads[j][0].wait()
        conv = jnp.dot(f[...], w[:, cols(j)], preferred_element_type=F32)
        centre = jnp.sum(conv, axis=0, keepdims=True) / ROWS
        mid[:, cols(j)] = jnp.concatenate([conv - centre, blank], axis=0).astype(BF)
        stores.append(copy(mid.at[:, cols(j)], kept_any.at[pl.ds(TALL, TALL), cols(j)], sems.at[4, j]))
        loads[j][1].wait()
        loads[j][2].wait()
        u = kept_part(pre[:, cols(j)], cot[:, cols(j)])
        up[:, cols(j)] = u
        stores.append(copy(up.at[:, cols(j)], up_any.at[:, cols(j)], sems.at[3, j]))
        tall[:, cols(j)] = jnp.concatenate([u.astype(F32), blank], axis=0).astype(BF)
        stores.append(copy(tall.at[:, cols(j)], kept_any.at[pl.ds(0, TALL), cols(j)], sems.at[6, j]))
    for store in stores:
        store.wait()


def prep_call(features, weight, cotangent, pre_act):
    return pl.pallas_call(
        prep_kernel,
        in_specs=[ANY] * 4,
        out_specs=[ANY, ANY],
        out_shape=[
            jax.ShapeDtypeStruct((ROWS, C), BF),
            jax.ShapeDtypeStruct((KEPT, C), BF),
        ],
        scratch_shapes=[
            pltpu.VMEM((ROWS, CB), BF),
            pltpu.VMEM((CB, C), BF),
            pltpu.VMEM((ROWS, C), BF),
            pltpu.VMEM((ROWS, C), BF),
            pltpu.VMEM((ROWS, C), BF),
            pltpu.VMEM((TALL, C), BF),
            pltpu.VMEM((TALL, C), BF),
            pltpu.VMEM((CB // 4, C), BF),
            DMA((7, STEPS)),
        ],
        compiler_params=params(VMEM_ALL),
        cost_estimate=pl.CostEstimate(flops=3 * ROWS * CB * C, bytes_accessed=9000000, transcendentals=0),
        name="prep",
    )(features, weight, cotangent, pre_act)


def grad_of(up, mid, coef):
    return (coef[0:1] * (up.astype(F32) - coef[1:2]) - (mid.astype(F32) + coef[2:3]) * coef[3:4]).astype(BF)


def grad_kernel(
    stat, kept, bn, p0, p1, send, own, near_ref, coef_ref, ext_send, ext_own
):
    c, zh = lax.axis_index("c"), lax.axis_index("zh")
    up = kept.at[0:TALL]
    mid = kept.at[TALL : 2 * TALL]
    mine, far = p0[...].astype(F32), p1[...].astype(F32)
    low = jnp.where(zh == 0, mine, far)
    high = jnp.where(zh == 0, far, mine)
    near_ref[...] = jnp.concatenate([low, high], axis=0).astype(BF)
    sums = jnp.sum(stat[...], axis=0)
    mean = sums[0:1] / COUNT
    inv_std = lax.rsqrt(sums[1:2] / COUNT - mean * mean + eps_norm)
    sum_b = sums[2:3]
    sum_g = inv_std * (sums[3:4] - mean * sum_b)
    alpha = bn[0:1] * inv_std
    slope = alpha * inv_std * (sum_g / COUNT)
    shift = sum_b / COUNT
    centre = stat[4 * zh + lax.axis_index("x")][0:1] / ROWS
    coef = jnp.concatenate([alpha, shift, centre - mean, slope], axis=0)
    coef_ref[...] = coef
    scale_row = sum_g * 0.125
    shift_row = sum_b * 0.125
    mine = jnp.where(c == 0, scale_row, shift_row)
    other = jnp.where(c == 0, shift_row, scale_row)
    ext_send[...] = jnp.zeros_like(ext_send)
    ext_own[...] = jnp.zeros_like(ext_own)
    for q in range(16):
        ext_own[16 * q : 16 * q + 1, :] = mine[:, 128 * q : 128 * q + 128]
        ext_send[16 * q : 16 * q + 1, :] = other[:, 128 * q : 128 * q + 128]
    own[:, C:] = ext_own[...].astype(BF)
    send[:, C:] = ext_send[...].astype(BF)
    ft = jnp.concatenate([kept[2 * TALL :, CB * b : CB * b + TALL] for b in range(4)], axis=0)
    for j in range(STEPS):
        at = slice(j * COLS, j * COLS + COLS)
        g = jnp.dot(ft, grad_of(up[:, at], mid[:, at], coef[:, at]), preferred_element_type=F32)
        send[:, at] = g[CB // 2 :].astype(BF)
        own[:, at] = g[: CB // 2].astype(BF)


def grad_call(stats, kept, bn_params, pieces):
    return pl.pallas_call(
        grad_kernel,
        in_specs=[VMEM] * 5,
        out_specs=[VMEM] * 4,
        out_shape=[
            jax.ShapeDtypeStruct((CB // 2, WIDE), BF),
            jax.ShapeDtypeStruct((CB // 2, WIDE), BF),
            jax.ShapeDtypeStruct((4, PIECE), BF),
            jax.ShapeDtypeStruct((4, C), F32),
        ],
        scratch_shapes=[
            pltpu.VMEM((CB // 2, EXT), F32),
            pltpu.VMEM((CB // 2, EXT), F32),
        ],
        compiler_params=params(),
        cost_estimate=pl.CostEstimate(flops=2 * ROWS * CB * C, bytes_accessed=7000000, transcendentals=0),
        name="grad",
    )(stats, kept, bn_params, *pieces)


def input_kernel(w_any, kept_any, coef_any, after_ref, out_ref, token_ref, w, up, mid, coef, sems):
    done(token_ref)
    early = copy(coef_any, coef, sems.at[3, 0])
    loads = [
        [
            copy(w_any.at[:, cols(j)], w.at[:, cols(j)], sems.at[0, j]),
            copy(kept_any.at[pl.ds(0, TALL), cols(j)], up.at[:, cols(j)], sems.at[1, j]),
            copy(kept_any.at[pl.ds(TALL, TALL), cols(j)], mid.at[:, cols(j)], sems.at[2, j]),
        ]
        for j in range(STEPS)
    ]
    early.wait()
    total = None
    for j in range(STEPS):
        for load in loads[j]:
            load.wait()
        part = lax.dot_general(
            grad_of(up[:, cols(j)], mid[:, cols(j)], coef[:, cols(j)]),
            w[:, cols(j)],
            (((1,), (1,)), ((), ())),
            preferred_element_type=F32,
        )
        total = part if total is None else total + part
    out_ref[...] = total[:ROWS].astype(BF)


def input_call(weight, kept, coef, after):
    return pl.pallas_call(
        input_kernel,
        in_specs=[ANY] * 3 + [SMEM],
        out_specs=[VMEM, SMEM],
        out_shape=[jax.ShapeDtypeStruct((ROWS, CB), BF), TOKEN],
        scratch_shapes=[
            pltpu.VMEM((CB, C), BF),
            pltpu.VMEM((TALL, C), BF),
            pltpu.VMEM((TALL, C), BF),
            pltpu.VMEM((4, C), F32),
            DMA((4, STEPS)),
        ],
        compiler_params=params(VMEM_ALL),
        cost_estimate=pl.CostEstimate(flops=2 * ROWS * CB * C, bytes_accessed=5500000, transcendentals=0),
        name="ginput",
    )(weight, kept, coef, after)


def rows_kernel(n0, n1, n2, n3, after_ref, base_ref, w, four):
    zl = lax.axis_index("zl")
    halves = []
    for high in range(2):
        for k, block in enumerate((n0, n1, n2, n3)):
            four[2 * k : 2 * k + 2, :] = block[...].astype(F32)[2 * high : 2 * high + 2]
        halves.append(pltpu.roll(four[...], 2 * zl, 0))
    both = jnp.concatenate(halves, axis=0)
    w[:, :C] = both[:, C : 2 * C]
    w[:, C:] = both[:, 2 * C + EXT :]
    base_ref[:, :C] = both[:, :C].astype(BF)
    base_ref[:, C:] = both[:, 2 * C : 2 * C + EXT].astype(BF)


def rows_call(blocks, after):
    return pl.pallas_call(
        rows_kernel,
        in_specs=[VMEM] * 4 + [SMEM],
        out_specs=[VMEM, VMEM],
        out_shape=[jax.ShapeDtypeStruct((16, WIDE), BF), jax.ShapeDtypeStruct((16, WIDE), F32)],
        scratch_shapes=[pltpu.VMEM((8, PIECE), F32)],
        compiler_params=params(),
        cost_estimate=pl.CostEstimate(flops=16 * PIECE, bytes_accessed=500000, transcendentals=0),
        name="rows",
    )(*blocks, after)


def pair_kernel(own_ref, got_ref, out_ref, token_ref):
    done(token_ref)
    out_ref[...] = (own_ref[...].astype(F32) + got_ref[...].astype(F32)).astype(BF)


def pair_call(own, got):
    return pl.pallas_call(
        pair_kernel,
        in_specs=[VMEM] * 2,
        out_specs=[VMEM, SMEM],
        out_shape=[jax.ShapeDtypeStruct((256, WIDE), BF), TOKEN],
        compiler_params=params(),
        cost_estimate=pl.CostEstimate(flops=256 * WIDE, bytes_accessed=3300000, transcendentals=0),
        name="pair",
    )(own, got)


def plane_kernel(got_ref, b0, b1, b2, b3, out_ref, base_any, token_ref, sems):
    done(token_ref)
    x = lax.axis_index("x")
    stores = []
    for k, block in enumerate((b0, b1, b2, b3)):
        stores.append(copy(block, base_any.at[(x + k) & 3], sems.at[k]))
    total = jnp.sum(got_ref[...].astype(F32), axis=0).astype(BF)
    out_ref[...] = jnp.broadcast_to(total[None], out_ref.shape)
    for store in stores:
        store.wait()


def plane_call(got, bases):
    return pl.pallas_call(
        plane_kernel,
        in_specs=[VMEM] + [ANY] * 4,
        out_specs=[VMEM, ANY, SMEM],
        out_shape=[
            jax.ShapeDtypeStruct((8, 16, WIDE), BF),
            jax.ShapeDtypeStruct((4, 16, WIDE), BF),
            TOKEN,
        ],
        scratch_shapes=[DMA((4,))],
        compiler_params=params(),
        cost_estimate=pl.CostEstimate(flops=256 * WIDE, bytes_accessed=1700000, transcendentals=0),
        name="plane",
    )(got, *bases)


def column_kernel(got_ref, w, b1, b2, b3, out_ref, own_ref, token_ref):
    done(token_ref)
    z = 4 * lax.axis_index("zh") + lax.axis_index("zl")
    total = jnp.sum(got_ref[...].astype(F32), axis=0)
    g = total[:, :C]
    g_hi, g_lo = hi_lo(jnp.sum(g * g, axis=(0, 1), keepdims=True))
    w_hi, w_lo = hi_lo(jnp.sum(w[:, C:], axis=(0, 1), keepdims=True))
    row = lax.broadcasted_iota(jnp.int32, (16, EXT), 0)
    lane = lax.broadcasted_iota(jnp.int32, (16, EXT), 1)
    bn_hi, bn_lo = hi_lo(total[0:1, C:])
    ext = jnp.where(row == 0, bn_hi, jnp.where(row == 1, bn_lo, 0.0))
    for k, value in enumerate((g_hi, g_lo, w_hi, w_lo)):
        ext = jnp.where((row == 2) & (lane == k), value, ext)
    step = (g + decay_rate * w[:, :C]).astype(BF)
    out_ref[:, :, :C] = jnp.broadcast_to(step[None], (16, 16, C))
    out_ref[:, :, C:] = jnp.broadcast_to(ext.astype(BF)[None], (16, 16, EXT))
    own_ref[...] = pltpu.roll(g, (16 - 2 * z) & 15, 0)[0:2]


def column_call(got, w_rows, bases):
    return pl.pallas_call(
        column_kernel,
        in_specs=[VMEM] * 2 + [ANY] * 3,
        out_specs=[VMEM, VMEM, SMEM],
        out_shape=[
            jax.ShapeDtypeStruct((16, 16, WIDE), BF),
            jax.ShapeDtypeStruct((2, C), F32),
            TOKEN,
        ],
        compiler_params=params(),
        cost_estimate=pl.CostEstimate(flops=128 * WIDE, bytes_accessed=1700000, transcendentals=0),
        name="column",
    )(got, w_rows, *bases)


def basis_kernel(b0, b1, b2, b3, m_any, v_any, bnm_any, after_ref, input_ref, base_any, keep_ref, bnm, sems):
    y = lax.axis_index("y")
    stores = [
        copy(m_any, keep_ref.at[:, pl.ds(0, C)], sems.at[16]),
        copy(v_any, keep_ref.at[:, pl.ds(C, C)], sems.at[17]),
    ]
    load = copy(bnm_any, bnm, sems.at[18])
    for k, block in enumerate((b0, b1, b2, b3)):
        for x in range(4):
            stores.append(copy(block.at[x], base_any.at[4 * x + ((y + k) & 3)], sems.at[4 * k + x]))
    load.wait()
    keep_ref[:, 2 * C :] = jnp.concatenate([bnm[...]] * 16, axis=1)
    for store in stores:
        store.wait()


def basis_call(bases, master, momentum, bn_momentum, *after):
    return pl.pallas_call(
        basis_kernel,
        in_specs=[ANY] * 7 + [SMEM] * 2,
        out_specs=[ANY, VMEM],
        out_shape=[jax.ShapeDtypeStruct((16, 16, WIDE), BF), jax.ShapeDtypeStruct((2, 2 * C + EXT), F32)],
        scratch_shapes=[pltpu.VMEM((2, 8), F32), DMA((19,))],
        compiler_params=params(),
        cost_estimate=pl.CostEstimate(flops=0, bytes_accessed=2200000, transcendentals=0),
        name="basis",
    )(*bases, master, momentum, bn_momentum, *after)


def update_kernel(
    b0, b1, a0, a1, bn_v, g_v, keep,
    nw_any, nbn_ref, nm_ref, nv_ref, nbm_ref, nbv_ref,
    nw, sems,
):
    c = lax.axis_index("c")
    mine = place()
    rows = [pl.ds(64 * i, 64) for i in range(4)]
    r = lax.broadcasted_iota(jnp.int32, (128, 128), 0)
    t = lax.broadcasted_iota(jnp.int32, (128, 128), 1)
    want = (
        ((t >> 3) & 1) * 64 + ((t >> 1) & 3) * 16 + ((t >> 4) & 3) * 4 + (c ^ (t >> 6)) * 2 + (t & 1)
    )
    sel = jnp.where(r == want, 1.0, 0.0).astype(BF)

    e0 = b0[:, C:].astype(F32)
    e1 = b1[:, C:].astype(F32)
    row = lax.broadcasted_iota(jnp.int32, (256, EXT), 0) & 15
    lane = lax.broadcasted_iota(jnp.int32, (256, EXT), 1)
    both = jnp.where(row == 2, e0 + e1, 0.0)
    g_sq = jnp.sum(jnp.where(lane < 2, both, 0.0), axis=(0, 1), keepdims=True)
    w_sq = jnp.sum(jnp.where((lane == 2) | (lane == 3), both, 0.0), axis=(0, 1), keepdims=True)

    def rate_of(w_sq, g_sq):
        w_norm = jnp.sqrt(w_sq)
        return learn_rate * (trust_coef * w_norm / (jnp.sqrt(g_sq) + decay_rate * w_norm))

    rate = rate_of(w_sq, g_sq)
    stores = []
    for i in range(4):
        at = slice(64 * i, 64 * i + 64)
        new = jnp.concatenate(
            [
                (a0[at, :C].astype(F32) - rate * b0[at, :C].astype(F32)).astype(BF),
                (a1[at, :C].astype(F32) - rate * b1[at, :C].astype(F32)).astype(BF),
            ],
            axis=0,
        )
        new = jnp.dot(sel, new, preferred_element_type=F32).astype(BF)
        nw[at, :] = new[:64]
        nw[slice(256 + 64 * i, 320 + 64 * i), :] = new[64:]
        stores.append(copy(nw.at[rows[i]], nw_any.at[rows[i]], sems.at[0, i]))
        far_rows = pl.ds(256 + 64 * i, 64)
        stores.append(copy(nw.at[far_rows], nw_any.at[far_rows], sems.at[1, i]))

    def flat(e):
        return jnp.concatenate([e[16 * q : 16 * q + 1] + e[16 * q + 1 : 16 * q + 2] for q in range(16)], axis=1)

    near, far = flat(e0), flat(e1)
    bn_grad = jnp.concatenate([jnp.where(c == 0, near, far), jnp.where(c == 0, far, near)], axis=0)
    bn = bn_v[...]
    bn_rate = rate_of(
        jnp.sum(bn * bn, axis=1, keepdims=True), jnp.sum(bn_grad * bn_grad, axis=1, keepdims=True)
    )
    ends_a = a0[:, C:].astype(F32) + a1[:, C:].astype(F32)
    blocks = [None] * 16
    for x in range(4):
        rows_x = ends_a[64 * x : 64 * x + 16]
        for y in range(1, 4):
            rows_x = rows_x + ends_a[64 * x + 16 * y : 64 * x + 16 * y + 16]
        for high in range(2):
            for half in range(2):
                top = 8 * high + 4 * half
                blocks[8 * high + 2 * x + half] = rows_x[top : top + 2] + rows_x[top + 2 : top + 4]
    bn_base = jnp.concatenate(blocks, axis=1)
    nbn_ref[...] = (bn_base - bn_rate * (bn_grad + decay_rate * bn)).astype(BF)
    master = keep[:, 0:C]
    new_v = momentum_rate * keep[:, C : 2 * C] + rate * (g_v[...] + decay_rate * master)
    nv_ref[...] = new_v
    nm_ref[...] = master - new_v
    lane = lax.broadcasted_iota(jnp.int32, (2, EXT), 1)

    def own_eight(row):
        kept = jnp.where((lane >> 3) == (mine & 15), own_block(row, mine), 0.0)
        eight = kept[:, 0:8]
        for s in range(1, 16):
            eight = eight + kept[:, 8 * s : 8 * s + 8]
        return eight

    own_bn = own_eight(bn)
    new_bnv = momentum_rate * keep[:, 2 * C : 2 * C + 8] + bn_rate * (own_eight(bn_grad) + decay_rate * own_bn)
    nbv_ref[...] = new_bnv
    nbm_ref[...] = own_bn - new_bnv
    for store in stores:
        store.wait()


def update_call(b0, b1, a0, a1, bn_params, g_own, keep):
    small = [jax.ShapeDtypeStruct((2, C), F32)] * 2 + [jax.ShapeDtypeStruct((2, 8), F32)] * 2
    return pl.pallas_call(
        update_kernel,
        in_specs=[VMEM] * 7,
        out_specs=[ANY] + [VMEM] * 5,
        out_shape=[jax.ShapeDtypeStruct((CB, C), BF), jax.ShapeDtypeStruct((2, C), BF)] + small,
        scratch_shapes=[pltpu.VMEM((CB, C), BF), DMA((2, 4))],
        compiler_params=params(),
        cost_estimate=pl.CostEstimate(flops=2 * CB * 128 * C, bytes_accessed=6500000, transcendentals=0),
        name="update",
    )(b0, b1, a0, a1, bn_params, g_own, keep)


def exchange(block, axes):
    return lax.all_to_all(block, axes, 0, 0, tiled=True)


def shift_pairs(move):
    out = []
    for i in range(256):
        c, y, zl, x, zh = i & 1, (i >> 1) & 3, (i >> 3) & 3, (i >> 5) & 3, i >> 7
        x, y, z = move(x, y, 4 * zh + zl)
        out.append((i, ((((z >> 2) * 4 + x) * 4 + (z & 3)) * 4 + y) * 2 + c))
    return out


def ring(block, size, move):
    parts = [block]
    for k in range(1, size):
        parts.append(lax.ppermute(block, AXES, shift_pairs(functools.partial(move, size - k))))
    return parts


def shards(features, weight, cotangent, pre_act, bn_params, master, momentum, bn_momentum):
    swap = functools.partial(lax.ppermute, axis_name=AXES, perm=sibling_pairs())

    stats, piece = stats_call(
        features, weight, cotangent, pre_act, master, momentum, bn_params, bn_momentum
    )
    pieces = [piece, lax.ppermute(piece, AXES, shift_pairs(lambda x, y, z: (x, y, z ^ 4)))]
    later, stats = lax.optimization_barrier((features, stats))
    up, kept = prep_call(later, weight, cotangent, pre_act)
    stats = exchange(stats, GX)
    send, own, near, coef = grad_call(stats, kept, bn_params, pieces)
    half, token = pair_call(own, swap(send))
    blocks = ring(near, 4, lambda k, x, y, z: (x, y, (z & 4) + ((z + k) & 3)))
    base, w_rows = rows_call(blocks, token)
    bases = ring(base, 4, lambda k, x, y, z: ((x + k) % 4, y, z))
    part, base, token = plane_call(exchange(half.reshape(16, 16, WIDE), XY), bases)
    bases = ring(base, 4, lambda k, x, y, z: (x, (y + k) % 4, z))
    grad_input, ready = input_call(weight, kept, coef, token)
    step, g_own, token = column_call(exchange(part, Z), w_rows, bases[1:])
    a0, keep = basis_call(bases, master, momentum, bn_momentum, token, ready)
    a0 = a0.reshape(256, WIDE)
    a1 = swap(a0)
    b0 = exchange(step, XY).reshape(256, WIDE)
    b1 = swap(b0)
    new_weight, new_bn, new_master, new_momentum, new_bn_master, new_bn_momentum = update_call(
        b0, b1, a0, a1, bn_params, g_own, keep
    )
    return (grad_input, up, new_master, new_momentum, new_weight, new_bn_master, new_bn_momentum, new_bn)


def solution(mesh):
    fine = Mesh(mesh.devices.reshape(SIZES), AXES)
    rows = P(AXES, None)
    cols = P(None, AXES)
    return jax.shard_map(
        shards,
        mesh=fine,
        in_specs=(rows, P(), rows, rows, P(), rows, rows, cols),
        out_specs=(rows, rows, rows, rows, P(), cols, cols, P()),
        check_vma=False,
    )
```

```python
import functools

import jax
import jax.numpy as jnp
from jax import lax
from jax.experimental import pallas as pl
from jax.experimental.pallas import tpu as pltpu
from jax.sharding import Mesh, PartitionSpec as P

eps_norm = 1e-05
momentum_rate = 0.9
learn_rate = 4.0
trust_coef = 0.001
decay_rate = 5e-05

AXES = ("zh", "x", "zl", "y", "c")
SIZES = (2, 4, 4, 4, 2)
GX = ("zh", "x")
XY = ("x", "y")
Z = ("zh", "zl")
BF = jnp.bfloat16
F32 = jnp.float32

ROWS = 392
CB = 512
C = 2048
EXT = 128
WIDE = C + EXT
PIECE = 2 * C + 2 * EXT
COLS = 512
STEPS = C // COLS
STAT_COLS = 1024
STAT_STEPS = C // STAT_COLS
COUNT = float(ROWS * 8)
TALL = 400
KEPT = 2 * TALL + CB // 4
VMEM_BYTES = 24 * 1024 * 1024
VMEM_ALL = 60 * 1024 * 1024


def sibling_pairs():
    return [(i, i ^ 1) for i in range(256)]


def natural_row(t, c):
    cc = c ^ (t >> 8)
    return (
        ((t >> 3) & 1) * 256
        + ((t >> 6) & 3) * 64
        + ((t >> 1) & 3) * 16
        + ((t >> 4) & 3) * 4
        + cc * 2
        + (t & 1)
    )


def hi_lo(v):
    hi = v.astype(BF).astype(F32)
    return hi, v - hi


def params(limit=VMEM_BYTES):
    return pltpu.CompilerParams(vmem_limit_bytes=limit)


ANY = pl.BlockSpec(memory_space=pl.ANY)
VMEM = pl.BlockSpec(memory_space=pltpu.VMEM)
SMEM = pl.BlockSpec(memory_space=pltpu.SMEM)
DMA = pltpu.SemaphoreType.DMA


TOKEN = jax.ShapeDtypeStruct((1,), jnp.int32)


def done(token_ref):
    token_ref[0] = 0


def copy(src, dst, sem):
    made = pltpu.make_async_copy(src, dst, sem)
    made.start()
    return made


def cols(j):
    return pl.ds(j * COLS, COLS)


def stat_cols(j):
    return pl.ds(j * STAT_COLS, STAT_COLS)


def place():
    at = lax.axis_index("zh")
    for axis, size in zip(AXES[1:], SIZES[1:]):
        at = at * size + lax.axis_index(axis)
    return at


def own_block(row, mine):
    block = jnp.zeros((2, EXT), F32)
    for q in range(16):
        block = jnp.where((mine >> 4) == q, row[:, EXT * q : EXT * q + EXT], block)
    return block


def kept_part(pre, cot):
    return jnp.where(pre > 0, cot, jnp.zeros_like(cot))


def stats_kernel(
    f_any, w_any, cot_any, pre_any, m_any, v_any, bn_any, bnm_any,
    stat_ref, base_ref,
    f, w, cot, pre, master, momentum, bn, bnm, sems,
):
    mine = place()
    small = [
        copy(m_any, master, sems.at[1, STAT_STEPS]),
        copy(v_any, momentum, sems.at[2, STAT_STEPS]),
        copy(bn_any, bn, sems.at[3, STAT_STEPS]),
        copy(bnm_any, bnm, sems.at[4, 0]),
    ]
    first = copy(f_any, f, sems.at[0, STAT_STEPS])
    loads = []
    for j in range(STAT_STEPS):
        loads.append(
            [
                copy(w_any.at[:, stat_cols(j)], w.at[:, stat_cols(j)], sems.at[0, j]),
                copy(cot_any.at[:, stat_cols(j)], cot.at[:, stat_cols(j)], sems.at[1, j]),
                copy(pre_any.at[:, stat_cols(j)], pre.at[:, stat_cols(j)], sems.at[2, j]),
            ]
        )
    for load in small:
        load.wait()
    base_ref[:, 0:C] = (master[...] - momentum_rate * momentum[...]).astype(BF)
    base_ref[:, C : 2 * C] = master[...].astype(BF)
    own_bn = own_block(bn[...], mine)
    lane = lax.broadcasted_iota(jnp.int32, (2, EXT), 1)
    bn_base = own_bn - momentum_rate * jnp.concatenate([bnm[...]] * 16, axis=1)
    base_ref[:, 2 * C : 2 * C + EXT] = jnp.where((lane >> 3) == (mine & 15), bn_base, 0.0).astype(BF)
    square = jnp.sum(master[...] * master[...], axis=(0, 1), keepdims=True)
    row = lax.broadcasted_iota(jnp.int32, (2, EXT), 0)
    hi, lo = hi_lo(square)
    square = jnp.where(lane == 0, hi, jnp.where(lane == 1, lo, 0.0))
    base_ref[:, 2 * C + EXT :] = jnp.where(row == 0, square, 0.0).astype(BF)
    first.wait()
    for j in range(STAT_STEPS):
        loads[j][0].wait()
        conv = jnp.dot(f[...], w[:, stat_cols(j)], preferred_element_type=F32)
        loads[j][1].wait()
        loads[j][2].wait()
        u = kept_part(pre[:, stat_cols(j)], cot[:, stat_cols(j)]).astype(F32)
        stat = jnp.concatenate(
            [
                jnp.sum(conv, axis=0, keepdims=True),
                jnp.sum(conv * conv, axis=0, keepdims=True),
                jnp.sum(u, axis=0, keepdims=True),
                jnp.sum(u * conv, axis=0, keepdims=True),
            ],
            axis=0,
        )
        stat_ref[:, :, stat_cols(j)] = jnp.broadcast_to(stat[None], (8, 4, STAT_COLS))


def stats_call(features, weight, cotangent, pre_act, master, momentum, bn_params, bn_momentum):
    return pl.pallas_call(
        stats_kernel,
        in_specs=[ANY] * 8,
        out_specs=[VMEM, VMEM],
        out_shape=[
            jax.ShapeDtypeStruct((8, 4, C), F32),
            jax.ShapeDtypeStruct((2, PIECE), BF),
        ],
        scratch_shapes=[
            pltpu.VMEM((ROWS, CB), BF),
            pltpu.VMEM((CB, C), BF),
            pltpu.VMEM((ROWS, C), BF),
            pltpu.VMEM((ROWS, C), BF),
            pltpu.VMEM((2, C), F32),
            pltpu.VMEM((2, C), F32),
            pltpu.VMEM((2, C), F32),
            pltpu.VMEM((2, 8), F32),
            DMA((5, STAT_STEPS + 1)),
        ],
        compiler_params=params(VMEM_ALL),
        cost_estimate=pl.CostEstimate(flops=2 * ROWS * CB * C, bytes_accessed=7500000, transcendentals=0),
        name="stats",
    )(features, weight, cotangent, pre_act, master, momentum, bn_params, bn_momentum)


def prep_kernel(
    f_any, w_any, cot_any, pre_any, up_any, kept_any, f, w, cot, pre, up, tall, mid, ft, sems
):
    first = copy(f_any, f, sems.at[5, 0])
    loads = [
        [
            copy(w_any.at[:, cols(j)], w.at[:, cols(j)], sems.at[0, j]),
            copy(cot_any.at[:, cols(j)], cot.at[:, cols(j)], sems.at[1, j]),
            copy(pre_any.at[:, cols(j)], pre.at[:, cols(j)], sems.at[2, j]),
        ]
        for j in range(STEPS)
    ]
    t = lax.broadcasted_iota(jnp.int32, (CB, CB), 0)
    r = lax.broadcasted_iota(jnp.int32, (CB, CB), 1)
    sel = jnp.where(r == natural_row(t, lax.axis_index("c")), 1.0, 0.0).astype(BF)
    first.wait()
    ft[...] = jnp.zeros_like(ft)
    got = lax.dot_general(sel, f[...], (((1,), (1,)), ((), ())), preferred_element_type=F32).astype(BF)
    for b in range(4):
        ft[:, CB * b : CB * b + ROWS] = got[128 * b : 128 * b + 128]
    blank = jnp.zeros((TALL - ROWS, COLS), F32)
    stores = [copy(ft, kept_any.at[pl.ds(2 * TALL, CB // 4)], sems.at[5, 1])]
    for j in range(STEPS):
        loads[j][0].wait()
        conv = jnp.dot(f[...], w[:, cols(j)], preferred_element_type=F32)
        centre = jnp.sum(conv, axis=0, keepdims=True) / ROWS
        mid[:, cols(j)] = jnp.concatenate([conv - centre, blank], axis=0).astype(BF)
        stores.append(copy(mid.at[:, cols(j)], kept_any.at[pl.ds(TALL, TALL), cols(j)], sems.at[4, j]))
        loads[j][1].wait()
        loads[j][2].wait()
        u = kept_part(pre[:, cols(j)], cot[:, cols(j)])
        up[:, cols(j)] = u
        stores.append(copy(up.at[:, cols(j)], up_any.at[:, cols(j)], sems.at[3, j]))
        tall[:, cols(j)] = jnp.concatenate([u.astype(F32), blank], axis=0).astype(BF)
        stores.append(copy(tall.at[:, cols(j)], kept_any.at[pl.ds(0, TALL), cols(j)], sems.at[6, j]))
    for store in stores:
        store.wait()


def prep_call(features, weight, cotangent, pre_act):
    return pl.pallas_call(
        prep_kernel,
        in_specs=[ANY] * 4,
        out_specs=[ANY, ANY],
        out_shape=[
            jax.ShapeDtypeStruct((ROWS, C), BF),
            jax.ShapeDtypeStruct((KEPT, C), BF),
        ],
        scratch_shapes=[
            pltpu.VMEM((ROWS, CB), BF),
            pltpu.VMEM((CB, C), BF),
            pltpu.VMEM((ROWS, C), BF),
            pltpu.VMEM((ROWS, C), BF),
            pltpu.VMEM((ROWS, C), BF),
            pltpu.VMEM((TALL, C), BF),
            pltpu.VMEM((TALL, C), BF),
            pltpu.VMEM((CB // 4, C), BF),
            DMA((7, STEPS)),
        ],
        compiler_params=params(VMEM_ALL),
        cost_estimate=pl.CostEstimate(flops=3 * ROWS * CB * C, bytes_accessed=9000000, transcendentals=0),
        name="prep",
    )(features, weight, cotangent, pre_act)


def grad_of(up, mid, coef):
    return (coef[0:1] * (up.astype(F32) - coef[1:2]) - (mid.astype(F32) + coef[2:3]) * coef[3:4]).astype(BF)


def grad_kernel(
    stat, kept, bn, p0, p1, send, own, near_ref, coef_ref, ext_send, ext_own
):
    c, zh = lax.axis_index("c"), lax.axis_index("zh")
    up = kept.at[0:TALL]
    mid = kept.at[TALL : 2 * TALL]
    mine, far = p0[...].astype(F32), p1[...].astype(F32)
    even = (lax.axis_index("zl") & 1) == 0
    low = jnp.where(even, mine, far)
    high = jnp.where(even, far, mine)
    near_ref[...] = jnp.concatenate([low, high], axis=0).astype(BF)
    sums = jnp.sum(stat[...], axis=0)
    mean = sums[0:1] / COUNT
    inv_std = lax.rsqrt(sums[1:2] / COUNT - mean * mean + eps_norm)
    sum_b = sums[2:3]
    sum_g = inv_std * (sums[3:4] - mean * sum_b)
    alpha = bn[0:1] * inv_std
    slope = alpha * inv_std * (sum_g / COUNT)
    shift = sum_b / COUNT
    centre = stat[4 * zh + lax.axis_index("x")][0:1] / ROWS
    coef = jnp.concatenate([alpha, shift, centre - mean, slope], axis=0)
    coef_ref[...] = coef
    scale_row = sum_g * 0.125
    shift_row = sum_b * 0.125
    mine = jnp.where(c == 0, scale_row, shift_row)
    other = jnp.where(c == 0, shift_row, scale_row)
    ext_send[...] = jnp.zeros_like(ext_send)
    ext_own[...] = jnp.zeros_like(ext_own)
    for q in range(16):
        ext_own[16 * q : 16 * q + 1, :] = mine[:, 128 * q : 128 * q + 128]
        ext_send[16 * q : 16 * q + 1, :] = other[:, 128 * q : 128 * q + 128]
    own[:, C:] = ext_own[...].astype(BF)
    send[:, C:] = ext_send[...].astype(BF)
    ft = jnp.concatenate([kept[2 * TALL :, CB * b : CB * b + TALL] for b in range(4)], axis=0)
    for j in range(STEPS):
        at = slice(j * COLS, j * COLS + COLS)
        g = jnp.dot(ft, grad_of(up[:, at], mid[:, at], coef[:, at]), preferred_element_type=F32)
        send[:, at] = g[CB // 2 :].astype(BF)
        own[:, at] = g[: CB // 2].astype(BF)


def grad_call(stats, kept, bn_params, pieces):
    return pl.pallas_call(
        grad_kernel,
        in_specs=[VMEM] * 5,
        out_specs=[VMEM] * 4,
        out_shape=[
            jax.ShapeDtypeStruct((CB // 2, WIDE), BF),
            jax.ShapeDtypeStruct((CB // 2, WIDE), BF),
            jax.ShapeDtypeStruct((4, PIECE), BF),
            jax.ShapeDtypeStruct((4, C), F32),
        ],
        scratch_shapes=[
            pltpu.VMEM((CB // 2, EXT), F32),
            pltpu.VMEM((CB // 2, EXT), F32),
        ],
        compiler_params=params(),
        cost_estimate=pl.CostEstimate(flops=2 * ROWS * CB * C, bytes_accessed=7000000, transcendentals=0),
        name="grad",
    )(stats, kept, bn_params, *pieces)


def input_kernel(w_any, kept_any, coef_any, after_ref, out_ref, token_ref, w, up, mid, coef, sems):
    done(token_ref)
    early = copy(coef_any, coef, sems.at[3, 0])
    loads = [
        [
            copy(w_any.at[:, cols(j)], w.at[:, cols(j)], sems.at[0, j]),
            copy(kept_any.at[pl.ds(0, TALL), cols(j)], up.at[:, cols(j)], sems.at[1, j]),
            copy(kept_any.at[pl.ds(TALL, TALL), cols(j)], mid.at[:, cols(j)], sems.at[2, j]),
        ]
        for j in range(STEPS)
    ]
    early.wait()
    total = None
    for j in range(STEPS):
        for load in loads[j]:
            load.wait()
        part = lax.dot_general(
            grad_of(up[:, cols(j)], mid[:, cols(j)], coef[:, cols(j)]),
            w[:, cols(j)],
            (((1,), (1,)), ((), ())),
            preferred_element_type=F32,
        )
        total = part if total is None else total + part
    out_ref[...] = total[:ROWS].astype(BF)


def input_call(weight, kept, coef, after):
    return pl.pallas_call(
        input_kernel,
        in_specs=[ANY] * 3 + [SMEM],
        out_specs=[VMEM, SMEM],
        out_shape=[jax.ShapeDtypeStruct((ROWS, CB), BF), TOKEN],
        scratch_shapes=[
            pltpu.VMEM((CB, C), BF),
            pltpu.VMEM((TALL, C), BF),
            pltpu.VMEM((TALL, C), BF),
            pltpu.VMEM((4, C), F32),
            DMA((4, STEPS)),
        ],
        compiler_params=params(VMEM_ALL),
        cost_estimate=pl.CostEstimate(flops=2 * ROWS * CB * C, bytes_accessed=5500000, transcendentals=0),
        name="ginput",
    )(weight, kept, coef, after)


def rows_kernel(n0, n1, n2, n3, after_ref, base_ref, w, four):
    for k, block in enumerate((n0, n1, n2, n3)):
        four[4 * k : 4 * k + 4, :] = block[...].astype(F32)
    pair = 2 * lax.axis_index("zh") + (lax.axis_index("zl") >> 1)
    both = pltpu.roll(four[...], 4 * pair, 0)
    w[:, :C] = both[:, C : 2 * C]
    w[:, C:] = both[:, 2 * C + EXT :]
    base_ref[:, :C] = both[:, :C].astype(BF)
    base_ref[:, C:] = both[:, 2 * C : 2 * C + EXT].astype(BF)


def rows_call(blocks, after):
    return pl.pallas_call(
        rows_kernel,
        in_specs=[VMEM] * 4 + [SMEM],
        out_specs=[VMEM, VMEM],
        out_shape=[jax.ShapeDtypeStruct((16, WIDE), BF), jax.ShapeDtypeStruct((16, WIDE), F32)],
        scratch_shapes=[pltpu.VMEM((16, PIECE), F32)],
        compiler_params=params(),
        cost_estimate=pl.CostEstimate(flops=16 * PIECE, bytes_accessed=500000, transcendentals=0),
        name="rows",
    )(*blocks, after)


def pair_kernel(own_ref, got_ref, out_ref, token_ref):
    done(token_ref)
    out_ref[...] = (own_ref[...].astype(F32) + got_ref[...].astype(F32)).astype(BF)


def pair_call(own, got):
    return pl.pallas_call(
        pair_kernel,
        in_specs=[VMEM] * 2,
        out_specs=[VMEM, SMEM],
        out_shape=[jax.ShapeDtypeStruct((256, WIDE), BF), TOKEN],
        compiler_params=params(),
        cost_estimate=pl.CostEstimate(flops=256 * WIDE, bytes_accessed=3300000, transcendentals=0),
        name="pair",
    )(own, got)


def plane_kernel(got_ref, b0, b1, b2, b3, out_ref, base_any, token_ref, sems):
    done(token_ref)
    x = lax.axis_index("x")
    stores = []
    for k, block in enumerate((b0, b1, b2, b3)):
        stores.append(copy(block, base_any.at[(x + k) & 3], sems.at[k]))
    total = jnp.sum(got_ref[...].astype(F32), axis=0).astype(BF)
    out_ref[...] = jnp.broadcast_to(total[None], out_ref.shape)
    for store in stores:
        store.wait()


def plane_call(got, bases):
    return pl.pallas_call(
        plane_kernel,
        in_specs=[VMEM] + [ANY] * 4,
        out_specs=[VMEM, ANY, SMEM],
        out_shape=[
            jax.ShapeDtypeStruct((8, 16, WIDE), BF),
            jax.ShapeDtypeStruct((4, 16, WIDE), BF),
            TOKEN,
        ],
        scratch_shapes=[DMA((4,))],
        compiler_params=params(),
        cost_estimate=pl.CostEstimate(flops=256 * WIDE, bytes_accessed=1700000, transcendentals=0),
        name="plane",
    )(got, *bases)


def column_kernel(got_ref, w, b1, b2, b3, out_ref, own_ref, token_ref):
    done(token_ref)
    z = 4 * lax.axis_index("zh") + lax.axis_index("zl")
    total = jnp.sum(got_ref[...].astype(F32), axis=0)
    g = total[:, :C]
    g_hi, g_lo = hi_lo(jnp.sum(g * g, axis=(0, 1), keepdims=True))
    w_hi, w_lo = hi_lo(jnp.sum(w[:, C:], axis=(0, 1), keepdims=True))
    row = lax.broadcasted_iota(jnp.int32, (16, EXT), 0)
    lane = lax.broadcasted_iota(jnp.int32, (16, EXT), 1)
    bn_hi, bn_lo = hi_lo(total[0:1, C:])
    ext = jnp.where(row == 0, bn_hi, jnp.where(row == 1, bn_lo, 0.0))
    for k, value in enumerate((g_hi, g_lo, w_hi, w_lo)):
        ext = jnp.where((row == 2) & (lane == k), value, ext)
    step = (g + decay_rate * w[:, :C]).astype(BF)
    out_ref[:, :, :C] = jnp.broadcast_to(step[None], (16, 16, C))
    out_ref[:, :, C:] = jnp.broadcast_to(ext.astype(BF)[None], (16, 16, EXT))
    own_ref[...] = pltpu.roll(g, (16 - 2 * z) & 15, 0)[0:2]


def column_call(got, w_rows, bases):
    return pl.pallas_call(
        column_kernel,
        in_specs=[VMEM] * 2 + [ANY] * 3,
        out_specs=[VMEM, VMEM, SMEM],
        out_shape=[
            jax.ShapeDtypeStruct((16, 16, WIDE), BF),
            jax.ShapeDtypeStruct((2, C), F32),
            TOKEN,
        ],
        compiler_params=params(),
        cost_estimate=pl.CostEstimate(flops=128 * WIDE, bytes_accessed=1700000, transcendentals=0),
        name="column",
    )(got, w_rows, *bases)


def basis_kernel(b0, b1, b2, b3, m_any, v_any, bnm_any, after_ref, input_ref, base_any, keep_ref, bnm, sems):
    y = lax.axis_index("y")
    stores = [
        copy(m_any, keep_ref.at[:, pl.ds(0, C)], sems.at[16]),
        copy(v_any, keep_ref.at[:, pl.ds(C, C)], sems.at[17]),
    ]
    load = copy(bnm_any, bnm, sems.at[18])
    for k, block in enumerate((b0, b1, b2, b3)):
        for x in range(4):
            stores.append(copy(block.at[x], base_any.at[4 * x + ((y + k) & 3)], sems.at[4 * k + x]))
    load.wait()
    keep_ref[:, 2 * C :] = jnp.concatenate([bnm[...]] * 16, axis=1)
    for store in stores:
        store.wait()


def basis_call(bases, master, momentum, bn_momentum, *after):
    return pl.pallas_call(
        basis_kernel,
        in_specs=[ANY] * 7 + [SMEM] * 2,
        out_specs=[ANY, VMEM],
        out_shape=[jax.ShapeDtypeStruct((16, 16, WIDE), BF), jax.ShapeDtypeStruct((2, 2 * C + EXT), F32)],
        scratch_shapes=[pltpu.VMEM((2, 8), F32), DMA((19,))],
        compiler_params=params(),
        cost_estimate=pl.CostEstimate(flops=0, bytes_accessed=2200000, transcendentals=0),
        name="basis",
    )(*bases, master, momentum, bn_momentum, *after)


def update_kernel(
    b0, b1, a0, a1, bn_v, g_v, keep,
    nw_any, nbn_ref, nm_ref, nv_ref, nbm_ref, nbv_ref,
    nw, sems,
):
    c = lax.axis_index("c")
    mine = place()
    rows = [pl.ds(64 * i, 64) for i in range(4)]
    r = lax.broadcasted_iota(jnp.int32, (128, 128), 0)
    t = lax.broadcasted_iota(jnp.int32, (128, 128), 1)
    want = (
        ((t >> 3) & 1) * 64 + ((t >> 1) & 3) * 16 + ((t >> 4) & 3) * 4 + (c ^ (t >> 6)) * 2 + (t & 1)
    )
    sel = jnp.where(r == want, 1.0, 0.0).astype(BF)

    e0 = b0[:, C:].astype(F32)
    e1 = b1[:, C:].astype(F32)
    row = lax.broadcasted_iota(jnp.int32, (256, EXT), 0) & 15
    lane = lax.broadcasted_iota(jnp.int32, (256, EXT), 1)
    both = jnp.where(row == 2, e0 + e1, 0.0)
    g_sq = jnp.sum(jnp.where(lane < 2, both, 0.0), axis=(0, 1), keepdims=True)
    w_sq = jnp.sum(jnp.where((lane == 2) | (lane == 3), both, 0.0), axis=(0, 1), keepdims=True)

    def rate_of(w_sq, g_sq):
        w_norm = jnp.sqrt(w_sq)
        return learn_rate * (trust_coef * w_norm / (jnp.sqrt(g_sq) + decay_rate * w_norm))

    rate = rate_of(w_sq, g_sq)
    stores = []
    for i in range(4):
        at = slice(64 * i, 64 * i + 64)
        new = jnp.concatenate(
            [
                (a0[at, :C].astype(F32) - rate * b0[at, :C].astype(F32)).astype(BF),
                (a1[at, :C].astype(F32) - rate * b1[at, :C].astype(F32)).astype(BF),
            ],
            axis=0,
        )
        new = jnp.dot(sel, new, preferred_element_type=F32).astype(BF)
        nw[at, :] = new[:64]
        nw[slice(256 + 64 * i, 320 + 64 * i), :] = new[64:]
        stores.append(copy(nw.at[rows[i]], nw_any.at[rows[i]], sems.at[0, i]))
        far_rows = pl.ds(256 + 64 * i, 64)
        stores.append(copy(nw.at[far_rows], nw_any.at[far_rows], sems.at[1, i]))

    def flat(e):
        return jnp.concatenate([e[16 * q : 16 * q + 1] + e[16 * q + 1 : 16 * q + 2] for q in range(16)], axis=1)

    near, far = flat(e0), flat(e1)
    bn_grad = jnp.concatenate([jnp.where(c == 0, near, far), jnp.where(c == 0, far, near)], axis=0)
    bn = bn_v[...]
    bn_rate = rate_of(
        jnp.sum(bn * bn, axis=1, keepdims=True), jnp.sum(bn_grad * bn_grad, axis=1, keepdims=True)
    )
    ends_a = a0[:, C:].astype(F32) + a1[:, C:].astype(F32)
    blocks = [None] * 16
    for x in range(4):
        rows_x = ends_a[64 * x : 64 * x + 16]
        for y in range(1, 4):
            rows_x = rows_x + ends_a[64 * x + 16 * y : 64 * x + 16 * y + 16]
        for high in range(2):
            for half in range(2):
                top = 8 * high + 4 * half
                blocks[8 * high + 2 * x + half] = rows_x[top : top + 2] + rows_x[top + 2 : top + 4]
    bn_base = jnp.concatenate(blocks, axis=1)
    nbn_ref[...] = (bn_base - bn_rate * (bn_grad + decay_rate * bn)).astype(BF)
    master = keep[:, 0:C]
    new_v = momentum_rate * keep[:, C : 2 * C] + rate * (g_v[...] + decay_rate * master)
    nv_ref[...] = new_v
    nm_ref[...] = master - new_v
    lane = lax.broadcasted_iota(jnp.int32, (2, EXT), 1)

    def own_eight(row):
        kept = jnp.where((lane >> 3) == (mine & 15), own_block(row, mine), 0.0)
        eight = kept[:, 0:8]
        for s in range(1, 16):
            eight = eight + kept[:, 8 * s : 8 * s + 8]
        return eight

    own_bn = own_eight(bn)
    new_bnv = momentum_rate * keep[:, 2 * C : 2 * C + 8] + bn_rate * (own_eight(bn_grad) + decay_rate * own_bn)
    nbv_ref[...] = new_bnv
    nbm_ref[...] = own_bn - new_bnv
    for store in stores:
        store.wait()


def update_call(b0, b1, a0, a1, bn_params, g_own, keep):
    small = [jax.ShapeDtypeStruct((2, C), F32)] * 2 + [jax.ShapeDtypeStruct((2, 8), F32)] * 2
    return pl.pallas_call(
        update_kernel,
        in_specs=[VMEM] * 7,
        out_specs=[ANY] + [VMEM] * 5,
        out_shape=[jax.ShapeDtypeStruct((CB, C), BF), jax.ShapeDtypeStruct((2, C), BF)] + small,
        scratch_shapes=[pltpu.VMEM((CB, C), BF), DMA((2, 4))],
        compiler_params=params(),
        cost_estimate=pl.CostEstimate(flops=2 * CB * 128 * C, bytes_accessed=6500000, transcendentals=0),
        name="update",
    )(b0, b1, a0, a1, bn_params, g_own, keep)


def exchange(block, axes):
    return lax.all_to_all(block, axes, 0, 0, tiled=True)


def shift_pairs(move):
    out = []
    for i in range(256):
        c, y, zl, x, zh = i & 1, (i >> 1) & 3, (i >> 3) & 3, (i >> 5) & 3, i >> 7
        x, y, z = move(x, y, 4 * zh + zl)
        out.append((i, ((((z >> 2) * 4 + x) * 4 + (z & 3)) * 4 + y) * 2 + c))
    return out


def ring(block, size, move):
    parts = [block]
    for k in range(1, size):
        parts.append(lax.ppermute(block, AXES, shift_pairs(functools.partial(move, size - k))))
    return parts


def shards(features, weight, cotangent, pre_act, bn_params, master, momentum, bn_momentum):
    swap = functools.partial(lax.ppermute, axis_name=AXES, perm=sibling_pairs())

    stats, piece = stats_call(
        features, weight, cotangent, pre_act, master, momentum, bn_params, bn_momentum
    )
    pieces = [piece, lax.ppermute(piece, AXES, shift_pairs(lambda x, y, z: (x, y, z ^ 1)))]
    later, stats = lax.optimization_barrier((features, stats))
    up, kept = prep_call(later, weight, cotangent, pre_act)
    stats = exchange(stats, GX)
    send, own, near, coef = grad_call(stats, kept, bn_params, pieces)
    half, token = pair_call(own, swap(send))
    blocks = ring(near, 4, lambda k, x, y, z: (x, y, (z + 2 * k) & 7))
    base, w_rows = rows_call(blocks, token)
    bases = ring(base, 4, lambda k, x, y, z: ((x + k) % 4, y, z))
    part, base, token = plane_call(exchange(half.reshape(16, 16, WIDE), XY), bases)
    bases = ring(base, 4, lambda k, x, y, z: (x, (y + k) % 4, z))
    grad_input, ready = input_call(weight, kept, coef, token)
    step, g_own, token = column_call(exchange(part, Z), w_rows, bases[1:])
    a0, keep = basis_call(bases, master, momentum, bn_momentum, token, ready)
    a0 = a0.reshape(256, WIDE)
    a1 = swap(a0)
    b0 = exchange(step, XY).reshape(256, WIDE)
    b1 = swap(b0)
    new_weight, new_bn, new_master, new_momentum, new_bn_master, new_bn_momentum = update_call(
        b0, b1, a0, a1, bn_params, g_own, keep
    )
    return (grad_input, up, new_master, new_momentum, new_weight, new_bn_master, new_bn_momentum, new_bn)


def solution(mesh):
    fine = Mesh(mesh.devices.reshape(SIZES), AXES)
    rows = P(AXES, None)
    cols = P(None, AXES)
    return jax.shard_map(
        shards,
        mesh=fine,
        in_specs=(rows, P(), rows, rows, P(), rows, rows, cols),
        out_specs=(rows, rows, rows, rows, P(), cols, cols, P()),
        check_vma=False,
    )
```
